128 devices in a mesh: grp: 16 (over y, z), mem: 8 (over x, core).
Axes of the slice: x: 4, y: 4, z: 4, core: 2. Of those that a mesh axis runs over, the one named last changes fastest.
Arguments:
- embeds: bfloat16 [65536, 768], P(('grp', 'mem')), may hold values from -200 to 200
- cluster: int32 [65536], P(('grp', 'mem')), may hold values from 0 to 199
- dest: int32 [65536], P(('grp', 'mem')), may hold values from 0 to 1023, as said below
Outputs:
- best: float32 [65536], P(('grp', 'mem'))
The draws below stay inside these ranges and needn't reach their ends.
Inputs may be any that keep to these rules, and one draw needn't show every extreme that they name: The embeddings of one device name distinct slots; slot s belongs to device s // 8 of grp+mem (grp slowest). All embeddings of one cluster belong to devices of one grp index, that is one value of dest // 64. Each grp index has one spread cluster: exactly the slots with s % 8 < 2 hold it, on any member. Every other cluster's embeddings all go to slots of one device. In every draw some device has all 8 of its slots filled by every device.
All inputs are finite; a program needn't handle non-finite values.
Results may differ from the reference program's by a relative error of at most 0.00054.
Values may be sent and summed in bfloat16 or wider, within the bound.
No kernel may reach another device: no remote copies, remote signals or barrier semaphores. Data moves between devices by JAX's collectives and lax.ppermute only.
A program may use at most 64 MiB of HBM per device.

```python
import math
import jax
import jax.numpy as jnp
from jax import lax

D = 768
NCLUST = 200
ROW_DEV = 512
ROWS = 65536
CAP = 8
N_GRP = 16
N_MEM = 8
DEVICES = 128


def layout(key):
    devices = ROWS // ROW_DEV
    slots = devices * CAP
    span = N_MEM * CAP
    shared = max(1, CAP // 4)
    keys = jax.random.split(key, 3)
    target = jax.random.randint(keys[0], (), 0, devices).astype(jnp.int32)
    owners = jnp.arange(slots, dtype=jnp.int32) // CAP

    def pick(one_key):
        score = jax.random.permutation(one_key, slots).astype(jnp.int32)
        score = jnp.where(owners == target, -1, score)
        order = jnp.argsort(score, stable=True)
        return order[:ROW_DEV].astype(jnp.int32)
    dest = jax.vmap(pick)(jax.random.split(keys[1], devices)).reshape(ROWS)
    group = dest // span
    member = dest // CAP % N_MEM
    column = dest % CAP
    target_group = target // N_MEM
    target_member = target % N_MEM
    shift = jnp.mod(NCLUST - 1 - target_group, N_GRP)
    start = jnp.mod(group + shift, N_GRP)
    count = (NCLUST - 1 - start) // N_GRP + 1
    rotate = jnp.mod(target_member - (count - 2), N_MEM)
    first = 1 + jnp.mod(member - rotate, N_MEM)
    owned = (count - 1 - first) // N_MEM + 1
    draws = jax.random.randint(keys[2], (2, ROWS), 0, owned[None, :])
    chosen = jnp.min(draws, axis=0)
    chosen = jnp.where(dest == target * CAP + CAP - 1, owned - 1, chosen)
    index = jnp.where(column < shared, 0, first + N_MEM * chosen)
    cluster = (start + N_GRP * index).astype(jnp.int32)
    return (dest, cluster)


def draw_dest(key, part):
    return layout(key)[0]


def draw_cluster(key, part):
    return layout(key)[1]


def draw_embeds(key, part):
    dest, cluster = layout(key)
    key = jax.random.fold_in(key, 5)
    keys = jax.random.split(key, 4)
    centers = jax.random.normal(keys[0], (NCLUST, D), jnp.float32)
    pull = jax.random.uniform(keys[1], (ROWS, 1), jnp.float32, 0.2, 1.2)
    scale = jnp.exp(jax.random.uniform(keys[2], (ROWS, 1), jnp.float32, 0.0, math.log(10.0)))
    noise = jax.random.normal(keys[3], (ROWS, D), jnp.float32)
    values = scale * (pull * centers[cluster] + noise)
    return values.astype(jnp.bfloat16)


def setup_inputs(seed: int = 0) -> dict:
    key_list = jax.random.split(jax.random.key(seed), 4)
    embeds = draw_embeds(jax.random.fold_in(key_list[3], 71), 0)
    cluster = draw_cluster(jax.random.fold_in(key_list[3], 71), 0)
    dest = draw_dest(jax.random.fold_in(key_list[3], 71), 0)
    return {"embeds": embeds, "cluster": cluster, "dest": dest}


def normalize(embeds):
    values = embeds.astype(jnp.float32)
    return (values * lax.rsqrt(lax.optimization_barrier(jnp.sum(values * values, axis=1, keepdims=True)) + 1e-06)).astype(jnp.bfloat16)

def reference(embeds, cluster, dest):
    unit = normalize(embeds)
    span = N_MEM * CAP
    group_size = DEVICES * span
    source = (jnp.arange(ROWS) // ROW_DEV).astype(jnp.int32)
    group = (dest // span).astype(jnp.int32)
    place = (source * span + dest % span).astype(jnp.int32)
    buffers = jnp.zeros((N_GRP, group_size, D), jnp.bfloat16).at[group, place].set(unit)
    labels = jnp.full((N_GRP, group_size), -1, jnp.int32).at[group, place].set(cluster)
    block = span * 16
    positions = jnp.arange(group_size, dtype=jnp.int32)

    def one_group(pair):
        rows, ids = pair
        columns = rows.astype(jnp.float32)
        query_rows = columns.reshape(group_size // block, block, D)
        query_ids = ids.reshape(group_size // block, block)
        query_pos = positions.reshape(group_size // block, block)

        def one_block(triple):
            queries, qids, qpos = triple
            scores = jnp.dot(queries, columns.T, precision=lax.Precision.HIGHEST)
            same = (qids[:, None] == ids[None, :]) & (qpos[:, None] != positions[None, :])
            return lax.optimization_barrier(jnp.max(jnp.where(same, scores, jnp.float32(-1.0)), axis=1))
        return lax.map(one_block, (query_rows, query_ids, query_pos)).reshape(group_size)
    results = lax.map(one_group, (buffers, labels))
    return results[group, place]
```

```python
import functools

import jax
import jax.numpy as jnp
from jax import lax
from jax.experimental import pallas as pl
from jax.experimental.pallas import tpu as pltpu
from jax.sharding import PartitionSpec as P

CAP = 8
SHARED = 2
LANES = 128
EMPTY = 2.0
VMEM_LIMIT = 48 * 1024 * 1024
HIGHEST = lax.Precision.HIGHEST


def params():
    return pltpu.CompilerParams(vmem_limit_bytes=VMEM_LIMIT)


def dot_t(a, b):
    return lax.dot_general(a, b, (((1,), (1,)), ((), ())), preferred_element_type=jnp.float32)


def pack_kernel(embeds_ref, cluster_ref, dest_ref, out_ref, unit_ref):
    rows, width = embeds_ref.shape
    block = out_ref.shape[0]

    @pl.when(pl.program_id(0) == 0)
    def _():
        values = embeds_ref[...].astype(jnp.float32)
        total = jnp.sum(values * values, axis=1, keepdims=True)
        unit_ref[...] = (values * lax.rsqrt(total + 1e-06)).astype(jnp.bfloat16)

    slot = pl.program_id(0) * block + lax.broadcasted_iota(jnp.int32, (block, rows), 0)
    here = slot == dest_ref[...]
    pick = jnp.where(here, 1.0, 0.0).astype(jnp.bfloat16)
    labels = (cluster_ref[...] + 1).astype(jnp.float32)
    marks = jnp.where(here, labels, 0.0).astype(jnp.bfloat16)
    out_ref[:, :width] = jnp.dot(
        pick, unit_ref[...], preferred_element_type=jnp.float32
    ).astype(jnp.bfloat16)
    out_ref[:, width:] = jnp.dot(
        marks, jnp.ones((rows, LANES), jnp.bfloat16), preferred_element_type=jnp.float32
    ).astype(jnp.bfloat16)


def pack(embeds, cluster, dest, slots):
    rows, width = embeds.shape
    block = 256
    whole = lambda i: (0, 0)
    return pl.pallas_call(
        pack_kernel,
        grid=(slots // block,),
        out_shape=jax.ShapeDtypeStruct((slots, width + LANES), jnp.bfloat16),
        in_specs=[
            pl.BlockSpec((rows, width), whole),
            pl.BlockSpec((1, rows), whole),
            pl.BlockSpec((1, rows), whole),
        ],
        out_specs=pl.BlockSpec((block, width + LANES), lambda i: (i, 0)),
        scratch_shapes=[pltpu.VMEM((rows, width), jnp.bfloat16)],
        compiler_params=params(),
    )(embeds, cluster.reshape(1, rows), dest.reshape(1, rows))


def extract_kernel(rows_ref, out_ref):
    slots, wide = rows_ref.shape
    width = wide - LANES
    chunk = out_ref.shape[0]
    sources = slots // CAP
    row = lax.broadcasted_iota(jnp.int32, (chunk, slots), 0)
    want = (row % sources) * CAP + row // sources
    pick = jnp.where(lax.broadcasted_iota(jnp.int32, (chunk, slots), 1) == want, 1.0, 0.0)
    pick = pick.astype(jnp.bfloat16)
    picked = jnp.dot(pick, rows_ref[...], preferred_element_type=jnp.float32)
    empty = (picked[:, width:] == 0.0) & (
        lax.broadcasted_iota(jnp.int32, (chunk, LANES), 1) == 0
    )
    out_ref[:, :LANES] = jnp.where(empty, EMPTY, picked[:, :LANES]).astype(jnp.bfloat16)
    out_ref[:, LANES:] = picked[:, LANES:width].astype(jnp.bfloat16)


def extract(arrived, chunk):
    slots, wide = arrived.shape
    return pl.pallas_call(
        extract_kernel,
        out_shape=jax.ShapeDtypeStruct((chunk, wide - LANES), jnp.bfloat16),
        compiler_params=params(),
    )(arrived)


def local_kernel(rows_ref, out_ref):
    slots, wide = rows_ref.shape
    width = wide - LANES
    block = 256
    column_labels = dot_t(jnp.ones((8, LANES), jnp.bfloat16), rows_ref[:, width:])[:1] * (
        1.0 / LANES
    )
    eye = lax.broadcasted_iota(jnp.int32, (block, block), 0) == lax.broadcasted_iota(
        jnp.int32, (block, block), 1
    )
    for q in range(slots // block):
        queries = rows_ref[q * block : (q + 1) * block, :width]
        labels = column_labels[:, q * block : (q + 1) * block]
        best = jnp.full((1, block), -1.0, jnp.float32)
        for k in range(slots // block):
            keys = rows_ref[k * block : (k + 1) * block, :]
            scores = dot_t(keys[:, :width], queries)
            key_labels = keys[:, width : width + 1].astype(jnp.float32)
            same = key_labels == labels
            if k == q:
                same = same & ~eye
            best = jnp.maximum(
                best, jnp.max(jnp.where(same, scores, -1.0), axis=0, keepdims=True)
            )
        out_ref[:, q * block : (q + 1) * block] = best


def local_best(arrived):
    slots, wide = arrived.shape
    return pl.pallas_call(
        local_kernel,
        out_shape=jax.ShapeDtypeStruct((1, slots), jnp.float32),
        compiler_params=params(),
    )(arrived)


def spread_kernel(members, place_ref, local_ref, own_ref, other_ref, after_ref, before_ref, out_ref):
    chunk = own_ref.shape[0]
    sources = chunk // SHARED

    def best(keys_ref, queries_ref):
        scores = dot_t(keys_ref[...], queries_ref[...])
        filled = keys_ref[:, :1].astype(jnp.float32) < (1.0 + EMPTY) / 2
        return jnp.max(jnp.where(filled, scores, -1.0), axis=0, keepdims=True)

    own = jnp.maximum(best(other_ref, own_ref), best(after_ref, own_ref))
    other = best(after_ref, other_ref)
    before = best(after_ref, before_ref)
    after = jnp.maximum(
        jnp.maximum(best(own_ref, after_ref), best(other_ref, after_ref)),
        best(before_ref, after_ref),
    )
    parts = []
    lanes = []
    for index, values in enumerate((own, other, after, before)):
        values = jnp.maximum(values, -1.0) + 1.0
        member = place_ref[index]
        for j in range(SHARED):
            parts.append(values[:, j * sources : (j + 1) * sources])
            lanes.append(CAP + SHARED * member + j)
    stacked = jnp.concatenate(parts, axis=0)
    row = lax.broadcasted_iota(jnp.int32, (len(parts), LANES), 0)
    lane = lax.broadcasted_iota(jnp.int32, (len(parts), LANES), 1)
    target = jnp.zeros((len(parts), LANES), jnp.int32)
    for index, value in enumerate(lanes):
        target = jnp.where(row == index, value, target)
    place = jnp.where(lane == target, 1.0, 0.0)
    table = lax.dot_general(
        stacked, place, (((0,), (0,)), ((), ())), precision=HIGHEST,
        preferred_element_type=jnp.float32,
    )

    per = LANES // CAP
    source = lax.broadcasted_iota(jnp.int32, (sources, LANES), 0)
    lane = lax.broadcasted_iota(jnp.int32, (sources, LANES), 1)
    spots = [
        jnp.broadcast_to(local_ref[:, t * LANES : (t + 1) * LANES], (per, LANES))
        for t in range(sources // per)
    ]
    mine = jnp.where(lane // CAP == source % per, jnp.concatenate(spots, axis=0) + 1.0, 0.0)
    fold = jnp.where(source % CAP == lane, 1.0, 0.0)
    table = table + jnp.dot(
        mine, fold, precision=HIGHEST, preferred_element_type=jnp.float32
    )
    out_ref[...] = table - 1.0


def spread_best(place, local, own, other, after, before, members):
    sources = own.shape[0] // SHARED
    vmem = pl.BlockSpec(memory_space=pltpu.VMEM)
    return pl.pallas_call(
        functools.partial(spread_kernel, members),
        out_shape=jax.ShapeDtypeStruct((sources, LANES), jnp.float32),
        in_specs=[pl.BlockSpec(memory_space=pltpu.SMEM)] + [vmem] * 5,
        compiler_params=params(),
    )(place, local, own, other, after, before)


def lookup_kernel(members, table_ref, dest_ref, out_ref):
    devices = table_ref.shape[0]
    rows = dest_ref.shape[1]
    table = table_ref[...]
    grouped = table.reshape(devices // members, members, LANES)
    most = jnp.broadcast_to(jnp.max(grouped, axis=1, keepdims=True), grouped.shape)
    lane = lax.broadcasted_iota(jnp.int32, (devices, LANES), 1)
    table = jnp.where(lane < CAP, table, most.reshape(devices, LANES))
    dest = dest_ref[...]
    owner = dest // CAP
    column = dest % CAP
    pick = jnp.where(
        lax.broadcasted_iota(jnp.int32, (devices, rows), 0) == owner, 1.0, 0.0
    )
    found = lax.dot_general(
        table, pick, (((0,), (0,)), ((), ())), precision=HIGHEST,
        preferred_element_type=jnp.float32,
    )
    lane = lax.broadcasted_iota(jnp.int32, (LANES, rows), 0)
    shared = jnp.where(column < SHARED, CAP + SHARED * (owner % members) + column, column)
    wanted = (lane == column) | (lane == shared)
    out_ref[...] = jnp.max(jnp.where(wanted, found, -1.0), axis=0, keepdims=True)


def lookup(table, dest, members):
    rows = dest.shape[0]
    return pl.pallas_call(
        functools.partial(lookup_kernel, members),
        out_shape=jax.ShapeDtypeStruct((1, rows), jnp.float32),
        compiler_params=params(),
    )(table, dest.reshape(1, rows)).reshape(rows)


def neighbours(members):
    chips = members // 2
    other, after, before = [], [], []
    for chip in range(chips):
        for core in range(2):
            other.append(2 * chip + 1 - core)
            after.append(2 * ((chip + 1) % chips) + core)
            crossed = core if chip < chips // 2 else 1 - core
            before.append(2 * ((chip - 1) % chips) + crossed)
    return other, after, before


def shards(embeds, cluster, dest):
    members = lax.axis_size("mem")
    devices = lax.axis_size("grp") * members
    width = embeds.shape[1]
    slots = devices * CAP
    outgoing = pack(embeds, cluster, dest, slots)
    arrived = lax.all_to_all(
        outgoing.reshape(devices, CAP, width + LANES),
        ("grp", "mem"),
        split_axis=0,
        concat_axis=0,
        tiled=True,
    ).reshape(slots, width + LANES)
    own = extract(arrived, devices * SHARED)
    sources = neighbours(members)
    received = [
        lax.ppermute(own, "mem", [(s, d) for d, s in enumerate(source)]) for source in sources
    ]
    local = local_best(arrived)
    me = lax.axis_index("mem")
    place = jnp.stack([me] + [jnp.asarray(s, jnp.int32)[me] for s in sources]).astype(jnp.int32)
    table = spread_best(place, local, own, *received, members)
    returned = lax.all_to_all(
        table.reshape(devices, 1, LANES),
        ("grp", "mem"),
        split_axis=0,
        concat_axis=0,
        tiled=True,
    ).reshape(devices, LANES)
    return lookup(returned, dest, members)


def solution(mesh):
    placed = (P(("grp", "mem"), None), P(("grp", "mem")), P(("grp", "mem")))
    return jax.shard_map(
        shards, mesh=mesh, in_specs=placed, out_specs=P(("grp", "mem")), check_vma=False
    )
```

```python
import functools

import jax
import jax.numpy as jnp
from jax import lax
from jax.experimental import pallas as pl
from jax.experimental.pallas import tpu as pltpu
from jax.sharding import PartitionSpec as P

CAP = 8
SHARED = 2
LANES = 128
PARTS = 4
EMPTY = 2.0
VMEM_LIMIT = 48 * 1024 * 1024
HIGHEST = lax.Precision.HIGHEST


def params():
    return pltpu.CompilerParams(vmem_limit_bytes=VMEM_LIMIT)


def dot_t(a, b):
    return lax.dot_general(a, b, (((1,), (1,)), ((), ())), preferred_element_type=jnp.float32)


def pack_kernel(embeds_hbm, cluster_hbm, dest_hbm, out_ref, embeds_ref, cluster_ref, dest_ref, unit_ref, sems):
    rows, width = embeds_ref.shape
    slots = out_ref.shape[0]
    part = rows // PARTS
    small = [
        pltpu.make_async_copy(dest_hbm, dest_ref, sems.at[0]),
        pltpu.make_async_copy(cluster_hbm, cluster_ref, sems.at[1]),
    ]
    large = [
        pltpu.make_async_copy(
            embeds_hbm.at[pl.ds(p * part, part)],
            embeds_ref.at[pl.ds(p * part, part)],
            sems.at[2 + p],
        )
        for p in range(PARTS)
    ]
    for copy in small + large:
        copy.start()
    for copy in small:
        copy.wait()
    labels = jnp.broadcast_to((cluster_ref[...] + 1).astype(jnp.float32), (8, rows))
    first = lax.broadcasted_iota(jnp.int32, (8, rows), 0) == 0
    labels = jnp.where(first, labels, 0.0).astype(jnp.bfloat16)
    unit_ref[:, width:] = lax.dot_general(
        labels, jnp.ones((8, LANES), jnp.bfloat16), (((0,), (0,)), ((), ())),
        preferred_element_type=jnp.float32,
    ).astype(jnp.bfloat16)
    block = 256
    picks = []
    for b in range(slots // block):
        slot = b * block + lax.broadcasted_iota(jnp.int32, (block, rows), 0)
        picks.append(jnp.where(slot == dest_ref[...], 1.0, 0.0).astype(jnp.bfloat16))
    for p in range(PARTS):
        large[p].wait()
        values = embeds_ref[p * part : (p + 1) * part, :].astype(jnp.float32)
        total = jnp.sum(values * values, axis=1, keepdims=True)
        unit_ref[p * part : (p + 1) * part, :width] = (
            values * lax.rsqrt(total + 1e-06)
        ).astype(jnp.bfloat16)
    for b in range(slots // block):
        out_ref[b * block : (b + 1) * block, :] = jnp.dot(
            picks[b], unit_ref[...], preferred_element_type=jnp.float32
        ).astype(jnp.bfloat16)


def pack(embeds, cluster, dest, slots):
    rows, width = embeds.shape
    return pl.pallas_call(
        pack_kernel,
        out_shape=jax.ShapeDtypeStruct((slots, width + LANES), jnp.bfloat16),
        in_specs=[pl.BlockSpec(memory_space=pltpu.HBM)] * 3,
        scratch_shapes=[
            pltpu.VMEM((rows, width), jnp.bfloat16),
            pltpu.VMEM((1, rows), jnp.int32),
            pltpu.VMEM((1, rows), jnp.int32),
            pltpu.VMEM((rows, width + LANES), jnp.bfloat16),
            pltpu.SemaphoreType.DMA((2 + PARTS,)),
        ],
        compiler_params=params(),
    )(embeds, cluster.reshape(1, rows), dest.reshape(1, rows))


def extract_kernel(rows_ref, out_ref):
    slots, wide = rows_ref.shape
    width = wide - LANES
    chunk = out_ref.shape[0]
    sources = slots // CAP
    row = lax.broadcasted_iota(jnp.int32, (chunk, slots), 0)
    want = (row % sources) * CAP + row // sources
    pick = jnp.where(lax.broadcasted_iota(jnp.int32, (chunk, slots), 1) == want, 1.0, 0.0)
    pick = pick.astype(jnp.bfloat16)
    picked = jnp.dot(pick, rows_ref[...], preferred_element_type=jnp.float32)
    empty = (picked[:, width:] == 0.0) & (
        lax.broadcasted_iota(jnp.int32, (chunk, LANES), 1) == 0
    )
    out_ref[:, :LANES] = jnp.where(empty, EMPTY, picked[:, :LANES]).astype(jnp.bfloat16)
    out_ref[:, LANES:] = picked[:, LANES:width].astype(jnp.bfloat16)


def extract(arrived, chunk):
    slots, wide = arrived.shape
    return pl.pallas_call(
        extract_kernel,
        out_shape=jax.ShapeDtypeStruct((chunk, wide - LANES), jnp.bfloat16),
        compiler_params=params(),
    )(arrived)


def local_kernel(rows_ref, out_ref):
    slots, wide = rows_ref.shape
    width = wide - LANES
    block = 256
    column_labels = dot_t(jnp.ones((8, LANES), jnp.bfloat16), rows_ref[:, width:])[:1] * (
        1.0 / LANES
    )
    eye = lax.broadcasted_iota(jnp.int32, (block, block), 0) == lax.broadcasted_iota(
        jnp.int32, (block, block), 1
    )
    results = []
    for q in range(slots // block):
        queries = rows_ref[q * block : (q + 1) * block, :width]
        labels = column_labels[:, q * block : (q + 1) * block]
        best = jnp.full((1, block), -1.0, jnp.float32)
        for k in range(slots // block):
            keys = rows_ref[k * block : (k + 1) * block, :]
            scores = dot_t(keys[:, :width], queries)
            key_labels = keys[:, width : width + 1].astype(jnp.float32)
            same = key_labels == labels
            if k == q:
                same = same & ~eye
            best = jnp.maximum(
                best, jnp.max(jnp.where(same, scores, -1.0), axis=0, keepdims=True)
            )
        results.append(best)
    local = jnp.concatenate(results, axis=1)
    sources = slots // CAP
    per = LANES // CAP
    source = lax.broadcasted_iota(jnp.int32, (sources, LANES), 0)
    lane = lax.broadcasted_iota(jnp.int32, (sources, LANES), 1)
    spots = [
        jnp.broadcast_to(local[:, t * LANES : (t + 1) * LANES], (per, LANES))
        for t in range(sources // per)
    ]
    mine = jnp.where(lane // CAP == source % per, jnp.concatenate(spots, axis=0) + 1.0, 0.0)
    fold = jnp.where(source % CAP == lane, 1.0, 0.0)
    out_ref[...] = jnp.dot(
        mine, fold, precision=HIGHEST, preferred_element_type=jnp.float32
    ) - 1.0


def local_best(arrived):
    slots, wide = arrived.shape
    return pl.pallas_call(
        local_kernel,
        out_shape=jax.ShapeDtypeStruct((slots // CAP, LANES), jnp.float32),
        compiler_params=params(),
    )(arrived)


def spread_kernel(members, local_ref, own_ref, other_ref, after_ref, before_ref, out_ref):
    chunk = own_ref.shape[0]
    sources = chunk // SHARED

    def best(keys_ref, queries_ref):
        scores = dot_t(keys_ref[...], queries_ref[...])
        filled = keys_ref[:, :1].astype(jnp.float32) < (1.0 + EMPTY) / 2
        return jnp.max(jnp.where(filled, scores, -1.0), axis=0, keepdims=True)

    own = jnp.maximum(best(other_ref, own_ref), best(after_ref, own_ref))
    other = best(after_ref, other_ref)
    before = best(after_ref, before_ref)
    after = jnp.maximum(
        jnp.maximum(best(own_ref, after_ref), best(other_ref, after_ref)),
        best(before_ref, after_ref),
    )
    places = held(lax.axis_index("mem"), members)
    parts = []
    lanes = []
    for index, values in enumerate((own, other, after, before)):
        values = jnp.maximum(values, -1.0) + 1.0
        member = places[index]
        for j in range(SHARED):
            parts.append(values[:, j * sources : (j + 1) * sources])
            lanes.append(CAP + SHARED * member + j)
    stacked = jnp.concatenate(parts, axis=0)
    row = lax.broadcasted_iota(jnp.int32, (len(parts), LANES), 0)
    lane = lax.broadcasted_iota(jnp.int32, (len(parts), LANES), 1)
    target = jnp.zeros((len(parts), LANES), jnp.int32)
    for index, value in enumerate(lanes):
        target = jnp.where(row == index, value, target)
    place = jnp.where(lane == target, 1.0, 0.0)
    table = lax.dot_general(
        stacked, place, (((0,), (0,)), ((), ())), precision=HIGHEST,
        preferred_element_type=jnp.float32,
    )

    out_ref[...] = table + local_ref[...]


def spread_best(local, own, other, after, before, members):
    sources = own.shape[0] // SHARED
    vmem = pl.BlockSpec(memory_space=pltpu.VMEM)
    return pl.pallas_call(
        functools.partial(spread_kernel, members),
        out_shape=jax.ShapeDtypeStruct((sources, LANES), jnp.float32),
        in_specs=[vmem] * 5,
        compiler_params=params(),
    )(local, own, other, after, before)


def lookup_kernel(members, table_ref, dest_ref, out_ref):
    devices = table_ref.shape[0]
    rows = dest_ref.shape[1]
    table = table_ref[...]
    grouped = table.reshape(devices // members, members, LANES)
    most = jnp.broadcast_to(jnp.max(grouped, axis=1, keepdims=True), grouped.shape)
    lane = lax.broadcasted_iota(jnp.int32, (devices, LANES), 1)
    table = jnp.where(lane < CAP, table, most.reshape(devices, LANES))
    dest = dest_ref[...]
    owner = dest // CAP
    column = dest % CAP
    pick = jnp.where(
        lax.broadcasted_iota(jnp.int32, (devices, rows), 0) == owner, 1.0, 0.0
    )
    found = lax.dot_general(
        table, pick, (((0,), (0,)), ((), ())), precision=HIGHEST,
        preferred_element_type=jnp.float32,
    )
    lane = lax.broadcasted_iota(jnp.int32, (LANES, rows), 0)
    shared = jnp.where(column < SHARED, CAP + SHARED * (owner % members) + column, column)
    wanted = (lane == column) | (lane == shared)
    out_ref[...] = jnp.max(jnp.where(wanted, found, -1.0), axis=0, keepdims=True)


def lookup(table, dest, members):
    rows = dest.shape[0]
    return pl.pallas_call(
        functools.partial(lookup_kernel, members),
        out_shape=jax.ShapeDtypeStruct((1, rows), jnp.float32),
        compiler_params=params(),
    )(table, dest.reshape(1, rows)).reshape(rows)


def held(me, members):
    chips = members // 2
    chip, core = me // 2, me % 2
    crossed = (chip // (chips // 2) + core) % 2
    return (
        me,
        2 * chip + 1 - core,
        2 * ((chip + 1) % chips) + core,
        2 * ((chip + chips - 1) % chips) + crossed,
    )


def shards(embeds, cluster, dest):
    members = lax.axis_size("mem")
    devices = lax.axis_size("grp") * members
    width = embeds.shape[1]
    slots = devices * CAP
    outgoing = pack(embeds, cluster, dest, slots)
    arrived = lax.all_to_all(
        outgoing.reshape(devices, CAP, width + LANES),
        ("grp", "mem"),
        split_axis=0,
        concat_axis=0,
        tiled=True,
    ).reshape(slots, width + LANES)
    own = extract(arrived, devices * SHARED)
    received = [
        lax.ppermute(own, "mem", [(held(m, members)[i], m) for m in range(members)])
        for i in (1, 2, 3)
    ]
    local = local_best(arrived)
    table = spread_best(local, own, *received, members)
    returned = lax.all_to_all(
        table.reshape(devices, 1, LANES),
        ("grp", "mem"),
        split_axis=0,
        concat_axis=0,
        tiled=True,
    ).reshape(devices, LANES)
    return lookup(returned, dest, members)


def solution(mesh):
    placed = (P(("grp", "mem"), None), P(("grp", "mem")), P(("grp", "mem")))
    return jax.shard_map(
        shards, mesh=mesh, in_specs=placed, out_specs=P(("grp", "mem")), check_vma=False
    )
```

```python
import functools

import jax
import jax.numpy as jnp
from jax import lax
from jax.experimental import pallas as pl
from jax.experimental.pallas import tpu as pltpu
from jax.sharding import PartitionSpec as P

CAP = 8
SHARED = 2
KEPT = CAP - SHARED
SPLIT = KEPT // 2
LANES = 128
VMEM_LIMIT = 48 * 1024 * 1024
HIGHEST = lax.Precision.HIGHEST


def place(dest, members):
    owner = dest // CAP
    group = owner // members
    member = owner % members
    column = dest % CAP
    shared = member * SHARED + column
    index = column - SHARED
    third = member % 3
    halved = third == 2
    spread = column < SHARED
    core = jnp.where(
        spread, shared // CAP, jnp.where(halved, index // SPLIT, third)
    )
    chip = jnp.where(spread, 0, 1 + member // 3)
    row = jnp.where(
        spread, shared % CAP, jnp.where(halved, index % SPLIT, index + SPLIT)
    )
    return group * members + 2 * chip + core, row


def params():
    return pltpu.CompilerParams(vmem_limit_bytes=VMEM_LIMIT)


def iota(shape, axis):
    return lax.broadcasted_iota(jnp.int32, shape, axis)


def dot(a, b):
    return jnp.dot(a, b, preferred_element_type=jnp.float32)


def dot_t(a, b):
    return lax.dot_general(a, b, (((1,), (1,)), ((), ())), preferred_element_type=jnp.float32)


def ones_where(mask):
    return jnp.where(mask, 1.0, 0.0).astype(jnp.bfloat16)


def pack_kernel(members, embeds_ref, packed_ref, out_ref, unit_ref, last_ref):
    rows, width = embeds_ref.shape
    slots = out_ref.shape[0]
    devices = slots // CAP
    packed = packed_ref[...]
    label = (packed // slots).astype(jnp.float32)
    device, row = place(packed % slots, members)
    slot = jnp.where(row < CAP, device * CAP + row, -1)

    values = embeds_ref[...].astype(jnp.float32)
    total = jnp.sum(values * values, axis=1, keepdims=True)
    unit_ref[...] = (values * lax.rsqrt(total + 1e-06)).astype(jnp.bfloat16)

    here = iota((devices, rows), 0) == device
    ninth = dot(ones_where(here & (row == CAP)), unit_ref[...])
    for piece in range(width // LANES):
        last_ref[pl.ds(piece, devices, stride=CAP), :] = ninth[
            :, piece * LANES : (piece + 1) * LANES
        ]
    marks = jnp.where(iota((LANES, rows), 0) == row, label, 0.0).astype(jnp.bfloat16)
    labels = dot_t(ones_where(here), marks)
    for piece in range(width // LANES, CAP):
        last_ref[pl.ds(piece, devices, stride=CAP), :] = labels
    out_ref[:, width:] = last_ref[...].astype(jnp.bfloat16)

    block = 256
    for b in range(slots // block):
        pick = ones_where(b * block + iota((block, rows), 0) == slot)
        out_ref[b * block : (b + 1) * block, :width] = dot(pick, unit_ref[...]).astype(
            jnp.bfloat16
        )


def pack(embeds, cluster, dest, slots, members):
    rows, width = embeds.shape
    packed = (dest + slots * (cluster + 1)).reshape(1, rows)
    return pl.pallas_call(
        functools.partial(pack_kernel, members),
        out_shape=jax.ShapeDtypeStruct((slots, width + LANES), jnp.bfloat16),
        scratch_shapes=[
            pltpu.VMEM((rows, width), jnp.bfloat16),
            pltpu.VMEM((slots, LANES), jnp.float32),
        ],
        compiler_params=params(),
    )(embeds, packed)


def spread_labels(labels, slots):
    row = iota((slots, LANES), 0)
    lane = iota((slots, LANES), 1)
    repeat = ones_where(row // CAP == lane)
    return jnp.where(lane == row % CAP, dot(repeat, labels.astype(jnp.bfloat16)), 0.0).astype(
        jnp.bfloat16
    )


def fold_block(best, keys, queries, key_labels, query_labels, skip=None):
    same = key_labels == query_labels
    if skip is not None:
        same = same & ~skip
    return jnp.maximum(
        best, jnp.max(jnp.where(same, dot_t(keys, queries), -1.0), axis=0, keepdims=True)
    )


def own_kernel(rows_ref, best_ref, labels_ref, last_ref, ninth_ref, column_ref):
    slots, wide = rows_ref.shape
    width = wide - LANES
    sources = slots // CAP
    last_ref[...] = rows_ref[:, width:].astype(jnp.float32)
    for piece in range(width // LANES):
        ninth_ref[:, piece * LANES : (piece + 1) * LANES] = last_ref[
            pl.ds(piece, sources, stride=CAP), :
        ].astype(jnp.bfloat16)
    labels = last_ref[pl.ds(width // LANES, sources, stride=CAP), :]
    spots = spread_labels(labels, slots)
    ones = jnp.ones((LANES, LANES), jnp.bfloat16)
    column_ref[:slots, :] = dot(spots, ones)
    at_ninth = ones_where(iota((LANES, LANES), 0) == CAP)
    column_ref[slots:, :] = dot(labels.astype(jnp.bfloat16), at_ninth)
    at_ninth = ones_where(iota((CAP, LANES), 1) == CAP)
    row_labels = jnp.concatenate(
        [dot_t(ones[:CAP], spots), dot_t(at_ninth, labels.astype(jnp.bfloat16))], axis=1
    )
    labels_ref[...] = row_labels

    block = 256
    starts = list(range(0, slots, block)) + [slots]
    sizes = [block] * (slots // block) + [sources]

    def read(i):
        if starts[i] == slots:
            return ninth_ref[...]
        return rows_ref[starts[i] : starts[i] + block, :width]

    for q, (query, size) in enumerate(zip(starts, sizes)):
        best = jnp.full((1, size), -1.0, jnp.float32)
        queries = read(q)
        for k, (key, count) in enumerate(zip(starts, sizes)):
            skip = None
            if k == q:
                skip = iota((count, size), 0) == iota((count, size), 1)
            best = fold_block(
                best,
                read(k),
                queries,
                column_ref[key : key + count, :1],
                row_labels[:1, query : query + size],
                skip,
            )
        best_ref[:, query : query + size] = best


def own_best(arrived):
    slots, wide = arrived.shape
    count = slots + slots // CAP
    return pl.pallas_call(
        own_kernel,
        out_shape=(
            jax.ShapeDtypeStruct((1, count), jnp.float32),
            jax.ShapeDtypeStruct((CAP, count), jnp.float32),
        ),
        scratch_shapes=[
            pltpu.VMEM((slots, LANES), jnp.float32),
            pltpu.VMEM((slots // CAP, wide - LANES), jnp.bfloat16),
            pltpu.VMEM((count, LANES), jnp.float32),
        ],
        compiler_params=params(),
    )(arrived)


def cross_kernel(best_ref, labels_ref, rows_ref, other_ref, out_ref, last_ref, column_ref):
    slots, wide = rows_ref.shape
    width = wide - LANES
    sources = slots // CAP
    last_ref[...] = other_ref[:, width:].astype(jnp.float32)
    labels = last_ref[pl.ds(width // LANES, sources, stride=CAP), :]
    column_ref[...] = dot(
        spread_labels(labels, slots), jnp.ones((LANES, LANES), jnp.bfloat16)
    )
    block = 256
    results = []
    for q in range(0, slots, block):
        best = best_ref[:, q : q + block]
        for k in range(0, slots, block):
            best = fold_block(
                best,
                other_ref[k : k + block, :width],
                rows_ref[q : q + block, :width],
                column_ref[k : k + block, :1],
                labels_ref[:1, q : q + block],
            )
        results.append(best)
    local = jnp.concatenate(results, axis=1)

    per = LANES // CAP
    source = iota((sources, LANES), 0)
    lane = iota((sources, LANES), 1)
    spots = jnp.concatenate(
        [
            jnp.broadcast_to(local[:, t * LANES : (t + 1) * LANES], (per, LANES))
            for t in range(sources // per)
        ],
        axis=0,
    )
    ninth = jnp.broadcast_to(best_ref[:, slots:], (sources, LANES))
    mine = jnp.concatenate(
        [
            jnp.where(lane // CAP == source % per, spots, 0.0),
            jnp.where(lane == source, ninth, 0.0),
        ],
        axis=1,
    )
    fold = jnp.concatenate(
        [
            jnp.where(iota((LANES, LANES), 0) % CAP == iota((LANES, LANES), 1), 1.0, 0.0),
            jnp.where(iota((LANES, LANES), 1) == CAP, 1.0, 0.0),
        ],
        axis=0,
    )
    out_ref[...] = jnp.dot(
        mine, fold, precision=HIGHEST, preferred_element_type=jnp.float32
    )


def cross_best(best, labels, arrived, other):
    slots = arrived.shape[0]
    return pl.pallas_call(
        cross_kernel,
        out_shape=jax.ShapeDtypeStruct((slots // CAP, LANES), jnp.float32),
        scratch_shapes=[
            pltpu.VMEM((slots, LANES), jnp.float32),
            pltpu.VMEM((slots, LANES), jnp.float32),
        ],
        compiler_params=params(),
    )(best, labels, arrived, other)


def lookup_kernel(members, table_ref, dest_ref, out_ref):
    devices = table_ref.shape[0]
    rows = dest_ref.shape[1]
    device, row = place(dest_ref[...], members)
    pick = jnp.where(iota((devices, rows), 0) == device, 1.0, 0.0)
    found = lax.dot_general(
        table_ref[...], pick, (((0,), (0,)), ((), ())), precision=HIGHEST,
        preferred_element_type=jnp.float32,
    )
    out_ref[...] = jnp.max(
        jnp.where(iota((LANES, rows), 0) == row, found, -1.0), axis=0, keepdims=True
    )


def lookup(table, dest, members):
    rows = dest.shape[0]
    return pl.pallas_call(
        functools.partial(lookup_kernel, members),
        out_shape=jax.ShapeDtypeStruct((1, rows), jnp.float32),
        compiler_params=params(),
    )(table, dest.reshape(1, rows)).reshape(rows)


def shards(embeds, cluster, dest):
    members = lax.axis_size("mem")
    devices = lax.axis_size("grp") * members
    width = embeds.shape[1]
    slots = devices * CAP
    outgoing = pack(embeds, cluster, dest, slots, members)
    arrived = lax.all_to_all(
        outgoing.reshape(devices, CAP, width + LANES),
        ("grp", "mem"),
        split_axis=0,
        concat_axis=0,
        tiled=True,
    ).reshape(slots, width + LANES)
    other = lax.ppermute(arrived, "mem", [(m, m ^ 1) for m in range(members)])
    best, labels = own_best(arrived)
    table = cross_best(best, labels, arrived, other)
    returned = lax.all_to_all(
        table.reshape(devices, 1, LANES),
        ("grp", "mem"),
        split_axis=0,
        concat_axis=0,
        tiled=True,
    ).reshape(devices, LANES)
    return lookup(returned, dest, members)


def solution(mesh):
    placed = (P(("grp", "mem"), None), P(("grp", "mem")), P(("grp", "mem")))
    return jax.shard_map(
        shards, mesh=mesh, in_specs=placed, out_specs=P(("grp", "mem")), check_vma=False
    )
```

```python
import functools

import jax
import jax.numpy as jnp
from jax import lax
from jax.experimental import pallas as pl
from jax.experimental.pallas import tpu as pltpu
from jax.sharding import PartitionSpec as P

CAP = 8
SHARED = 2
KEPT = CAP - SHARED
SPLIT = KEPT // 2
LANES = 128
VMEM_LIMIT = 48 * 1024 * 1024
HIGHEST = lax.Precision.HIGHEST


def place(dest, members):
    owner = dest // CAP
    group = owner // members
    member = owner % members
    column = dest % CAP
    shared = member * SHARED + column
    index = column - SHARED
    third = member % 3
    halved = third == 2
    spread = column < SHARED
    core = jnp.where(
        spread, shared // CAP, jnp.where(halved, index // SPLIT, third)
    )
    chip = jnp.where(spread, 0, 1 + member // 3)
    row = jnp.where(
        spread, shared % CAP, jnp.where(halved, index % SPLIT, index + SPLIT)
    )
    return group * members + 2 * chip + core, row


def params():
    return pltpu.CompilerParams(vmem_limit_bytes=VMEM_LIMIT)


def iota(shape, axis):
    return lax.broadcasted_iota(jnp.int32, shape, axis)


def dot(a, b):
    return jnp.dot(a, b, preferred_element_type=jnp.float32)


def dot_t(a, b):
    return lax.dot_general(a, b, (((1,), (1,)), ((), ())), preferred_element_type=jnp.float32)


def ones_where(mask):
    return jnp.where(mask, 1.0, 0.0).astype(jnp.bfloat16)


def pack_kernel(members, embeds_ref, packed_ref, out_ref, unit_ref, last_ref):
    rows, width = embeds_ref.shape
    slots = out_ref.shape[0]
    devices = slots // CAP
    packed = packed_ref[...]
    label = (packed // slots).astype(jnp.float32)
    device, row = place(packed % slots, members)
    slot = jnp.where(row < CAP, device * CAP + row, -1)

    values = embeds_ref[...].astype(jnp.float32)
    total = jnp.sum(values * values, axis=1, keepdims=True)
    unit_ref[...] = (values * lax.rsqrt(total + 1e-06)).astype(jnp.bfloat16)

    here = iota((devices, rows), 0) == device
    ninth = dot(ones_where(here & (row == CAP)), unit_ref[...])
    for piece in range(width // LANES):
        last_ref[pl.ds(piece, devices, stride=CAP), :] = ninth[
            :, piece * LANES : (piece + 1) * LANES
        ]
    marks = jnp.where(iota((LANES, rows), 0) == row, label, 0.0).astype(jnp.bfloat16)
    labels = dot_t(ones_where(here), marks)
    for piece in range(width // LANES, CAP):
        last_ref[pl.ds(piece, devices, stride=CAP), :] = labels
    out_ref[:, width:] = last_ref[...].astype(jnp.bfloat16)

    block = 256
    for b in range(slots // block):
        pick = ones_where(b * block + iota((block, rows), 0) == slot)
        out_ref[b * block : (b + 1) * block, :width] = dot(pick, unit_ref[...]).astype(
            jnp.bfloat16
        )


def pack(embeds, cluster, dest, slots, members):
    rows, width = embeds.shape
    packed = (dest + slots * (cluster + 1)).reshape(1, rows)
    return pl.pallas_call(
        functools.partial(pack_kernel, members),
        out_shape=jax.ShapeDtypeStruct((slots, width + LANES), jnp.bfloat16),
        scratch_shapes=[
            pltpu.VMEM((rows, width), jnp.bfloat16),
            pltpu.VMEM((slots, LANES), jnp.float32),
        ],
        compiler_params=params(),
    )(embeds, packed)


def ninth_lane(source):
    windows = LANES // CAP
    return CAP * ((source + 1) % windows) + source // windows


def spread_labels(labels, slots):
    row = iota((slots, LANES), 0)
    lane = iota((slots, LANES), 1)
    repeat = ones_where(row // CAP == lane)
    return jnp.where(lane == row % CAP, dot(repeat, labels), 0.0).astype(
        jnp.bfloat16
    )


def fold_block(best, keys, queries, key_labels, query_labels, skip=None):
    same = key_labels == query_labels
    if skip is not None:
        same = same & ~skip
    return jnp.maximum(
        best, jnp.max(jnp.where(same, dot_t(keys, queries), -1.0), axis=0, keepdims=True)
    )


def own_kernel(rows_ref, best_ref, labels_ref, last_ref, ninth_ref, column_ref):
    slots, wide = rows_ref.shape
    width = wide - LANES
    sources = slots // CAP
    last_ref[...] = rows_ref[:, width:].astype(jnp.float32)
    for piece in range(width // LANES):
        ninth_ref[:, piece * LANES : (piece + 1) * LANES] = last_ref[
            pl.ds(piece, sources, stride=CAP), :
        ].astype(jnp.bfloat16)
    labels = last_ref[pl.ds(width // LANES, sources, stride=CAP), :].astype(jnp.bfloat16)
    spots = spread_labels(labels, slots)
    order = ones_where(iota((sources, LANES), 0) == ninth_lane(iota((sources, LANES), 1)))
    ninth_ref[...] = dot(order, ninth_ref[...]).astype(jnp.bfloat16)
    labels = dot(order, labels).astype(jnp.bfloat16)
    ones = jnp.ones((LANES, LANES), jnp.bfloat16)
    column_ref[:slots, :] = dot(spots, ones)
    at_ninth = ones_where(iota((LANES, LANES), 0) == CAP)
    column_ref[slots:, :] = dot(labels, at_ninth)
    at_ninth = ones_where(iota((CAP, LANES), 1) == CAP)
    row_labels = jnp.concatenate(
        [dot_t(ones[:CAP], spots), dot_t(at_ninth, labels)], axis=1
    )
    labels_ref[...] = row_labels

    block = 256
    starts = list(range(0, slots, block)) + [slots]
    sizes = [block] * (slots // block) + [sources]

    def read(i):
        if starts[i] == slots:
            return ninth_ref[...]
        return rows_ref[starts[i] : starts[i] + block, :width]

    for q, (query, size) in enumerate(zip(starts, sizes)):
        best = jnp.full((1, size), -1.0, jnp.float32)
        queries = read(q)
        for k, (key, count) in enumerate(zip(starts, sizes)):
            skip = None
            if k == q:
                skip = iota((count, size), 0) == iota((count, size), 1)
            best = fold_block(
                best,
                read(k),
                queries,
                column_ref[key : key + count, :1],
                row_labels[:1, query : query + size],
                skip,
            )
        best_ref[:, query : query + size] = best


def own_best(arrived):
    slots, wide = arrived.shape
    count = slots + slots // CAP
    return pl.pallas_call(
        own_kernel,
        out_shape=(
            jax.ShapeDtypeStruct((1, count), jnp.float32),
            jax.ShapeDtypeStruct((CAP, count), jnp.float32),
        ),
        scratch_shapes=[
            pltpu.VMEM((slots, LANES), jnp.float32),
            pltpu.VMEM((slots // CAP, wide - LANES), jnp.bfloat16),
            pltpu.VMEM((count, LANES), jnp.float32),
        ],
        compiler_params=params(),
    )(arrived)


def cross_kernel(best_ref, labels_ref, rows_ref, other_ref, out_ref, last_ref, column_ref):
    slots, wide = rows_ref.shape
    width = wide - LANES
    sources = slots // CAP
    last_ref[...] = other_ref[:, width:].astype(jnp.float32)
    labels = last_ref[pl.ds(width // LANES, sources, stride=CAP), :].astype(jnp.bfloat16)
    column_ref[...] = dot(
        spread_labels(labels, slots), jnp.ones((LANES, LANES), jnp.bfloat16)
    )
    block = 256

    def run(last_key, first_query):
        own = [best_ref[:, q : q + block] for q in range(0, slots, block)]
        gained = [jnp.full((1, LANES), -1.0, jnp.float32)] * (slots // LANES)
        for k in range(0, last_key, block):
            widest = jnp.full((block, LANES), -1.0, jnp.float32)
            for q in range(first_query, slots, block):
                scores = dot_t(other_ref[k : k + block, :width], rows_ref[q : q + block, :width])
                same = column_ref[k : k + block, :1] == labels_ref[:1, q : q + block]
                scores = jnp.where(same, scores, -1.0)
                own[q // block] = jnp.maximum(
                    own[q // block], jnp.max(scores, axis=0, keepdims=True)
                )
                for lane in range(0, block, LANES):
                    widest = jnp.maximum(widest, scores[:, lane : lane + LANES])
            for j in range(0, block, LANES):
                gained[(k + j) // LANES] = jnp.max(
                    widest[j : j + LANES].T, axis=0, keepdims=True
                )
        windows = LANES // CAP
        own = jnp.concatenate(own, axis=1)
        tiles = range(slots // LANES)
        own = jnp.concatenate(
            [
                jnp.broadcast_to(own[:, t * LANES : (t + 1) * LANES], (windows, LANES))
                for t in tiles
            ],
            axis=0,
        )
        gained = jnp.concatenate(
            [jnp.broadcast_to(gained[t], (windows, LANES)) for t in tiles], axis=0
        )
        gained = pltpu.roll(gained, LANES // 2, 1)
        ninth = jnp.broadcast_to(best_ref[:, slots:], (sources, LANES))
        window = iota((sources, LANES), 1) // CAP
        mine = iota((sources, LANES), 0) % windows
        out_ref[...] = jnp.where(
            window == mine,
            own,
            jnp.where(window == (mine + windows // 2) % windows, gained, ninth),
        )

    core = lax.axis_index("mem") % 2

    @pl.when(core == 0)
    def _():
        run(slots // 2, 0)

    @pl.when(core == 1)
    def _():
        run(slots, slots // 2)


def cross_best(best, labels, arrived, other):
    slots = arrived.shape[0]
    return pl.pallas_call(
        cross_kernel,
        out_shape=jax.ShapeDtypeStruct((slots // CAP, LANES), jnp.float32),
        scratch_shapes=[
            pltpu.VMEM((slots, LANES), jnp.float32),
            pltpu.VMEM((slots, LANES), jnp.float32),
        ],
        compiler_params=params(),
    )(best, labels, arrived, other)


def lookup_kernel(members, table_ref, dest_ref, out_ref):
    devices = table_ref.shape[0]
    rows = dest_ref.shape[1]
    windows = LANES // CAP
    me = lax.axis_index("grp") * members + lax.axis_index("mem")
    mine = me % windows
    table = table_ref[...]
    turned = pltpu.roll(table, LANES // 2, 1)
    even = iota((devices, LANES), 0) % 2 == 0
    other = jnp.where(even, pltpu.roll(turned, devices - 1, 0), pltpu.roll(turned, 1, 0))
    window = iota((devices, LANES), 1) // CAP
    table = jnp.where(window == mine, jnp.maximum(table, other), table)
    device, row = place(dest_ref[...], members)
    pick = jnp.where(iota((devices, rows), 0) == device, 1.0, 0.0)
    found = lax.dot_general(
        table, pick, (((0,), (0,)), ((), ())), precision=HIGHEST,
        preferred_element_type=jnp.float32,
    )
    lane = jnp.where(row < CAP, CAP * mine + row, ninth_lane(me))
    out_ref[...] = jnp.max(
        jnp.where(iota((LANES, rows), 0) == lane, found, -1.0), axis=0, keepdims=True
    )


def lookup(table, dest, members):
    rows = dest.shape[0]
    return pl.pallas_call(
        functools.partial(lookup_kernel, members),
        out_shape=jax.ShapeDtypeStruct((1, rows), jnp.float32),
        compiler_params=params(),
    )(table, dest.reshape(1, rows)).reshape(rows)


def shards(embeds, cluster, dest):
    members = lax.axis_size("mem")
    devices = lax.axis_size("grp") * members
    width = embeds.shape[1]
    slots = devices * CAP
    outgoing = pack(embeds, cluster, dest, slots, members)
    arrived = lax.all_to_all(
        outgoing.reshape(devices, CAP, width + LANES),
        ("grp", "mem"),
        split_axis=0,
        concat_axis=0,
        tiled=True,
    ).reshape(slots, width + LANES)
    other = lax.ppermute(arrived, "mem", [(m, m ^ 1) for m in range(members)])
    best, labels = own_best(arrived)
    table = cross_best(best, labels, arrived, other)
    returned = lax.all_to_all(
        table.reshape(devices, 1, LANES),
        ("grp", "mem"),
        split_axis=0,
        concat_axis=0,
        tiled=True,
    ).reshape(devices, LANES)
    return lookup(returned, dest, members)


def solution(mesh):
    placed = (P(("grp", "mem"), None), P(("grp", "mem")), P(("grp", "mem")))
    return jax.shard_map(
        shards, mesh=mesh, in_specs=placed, out_specs=P(("grp", "mem")), check_vma=False
    )
```

```python
import functools

import jax
import jax.numpy as jnp
from jax import lax
from jax.experimental import pallas as pl
from jax.experimental.pallas import tpu as pltpu
from jax.sharding import PartitionSpec as P

CAP = 8
SHARED = 2
KEPT = CAP - SHARED
SPLIT = KEPT // 2
LANES = 128
VMEM_LIMIT = 48 * 1024 * 1024
HIGHEST = lax.Precision.HIGHEST


def place(dest, members):
    owner = dest // CAP
    group = owner // members
    member = owner % members
    column = dest % CAP
    shared = member * SHARED + column
    index = column - SHARED
    third = member % 3
    halved = third == 2
    spread = column < SHARED
    core = jnp.where(
        spread, shared // CAP, jnp.where(halved, index // SPLIT, third)
    )
    chip = jnp.where(spread, 0, 1 + member // 3)
    row = jnp.where(
        spread, shared % CAP, jnp.where(halved, index % SPLIT, index + SPLIT)
    )
    return group * members + 2 * chip + core, row


def params():
    return pltpu.CompilerParams(vmem_limit_bytes=VMEM_LIMIT)


def iota(shape, axis):
    return lax.broadcasted_iota(jnp.int32, shape, axis)


def dot(a, b):
    return jnp.dot(a, b, preferred_element_type=jnp.float32)


def dot_t(a, b):
    return lax.dot_general(a, b, (((1,), (1,)), ((), ())), preferred_element_type=jnp.float32)


def ones_where(mask):
    return jnp.where(mask, 1.0, 0.0).astype(jnp.bfloat16)


def pack_kernel(embeds_ref, packed_ref, pick_ref, out_ref, unit_ref, last_ref):
    rows, width = embeds_ref.shape
    slots = out_ref.shape[0]
    devices = slots // CAP
    packed = packed_ref[...]
    spot = packed % (2 * slots)
    label = (packed // (2 * slots)).astype(jnp.float32)
    device = jnp.where(spot < slots, spot // CAP, spot - slots)
    row = jnp.where(spot < slots, spot % CAP, CAP)

    values = embeds_ref[...].astype(jnp.float32)
    total = jnp.sum(values * values, axis=1, keepdims=True)
    unit_ref[...] = (values * lax.rsqrt(total + 1e-06)).astype(jnp.bfloat16)

    ninth = dot(pick_ref[slots:, :].astype(jnp.bfloat16), unit_ref[...])
    for piece in range(width // LANES):
        last_ref[pl.ds(piece, devices, stride=CAP), :] = ninth[
            :, piece * LANES : (piece + 1) * LANES
        ]
    here = ones_where(iota((devices, rows), 0) == device)
    marks = jnp.where(iota((LANES, rows), 0) == row, label, 0.0).astype(jnp.bfloat16)
    labels = dot_t(here, marks)
    for piece in range(width // LANES, CAP):
        last_ref[pl.ds(piece, devices, stride=CAP), :] = labels
    out_ref[:, width:] = last_ref[...].astype(jnp.bfloat16)

    block = 256
    for b in range(0, slots, block):
        out_ref[b : b + block, :width] = dot(pick_ref[b : b + block, :].astype(jnp.bfloat16), unit_ref[...]).astype(
            jnp.bfloat16
        )


def pack(embeds, cluster, dest, slots, members):
    rows, width = embeds.shape
    devices = slots // CAP
    device, row = place(dest, members)
    spot = jnp.where(row < CAP, device * CAP + row, slots + device)
    packed = (spot + 2 * slots * (cluster + 1)).reshape(1, rows)
    pick = jnp.where(iota((slots + devices, rows), 0) == spot[None], 1.0, 0.0)
    return pl.pallas_call(
        pack_kernel,
        out_shape=jax.ShapeDtypeStruct((slots, width + LANES), jnp.bfloat16),
        scratch_shapes=[
            pltpu.VMEM((rows, width), jnp.bfloat16),
            pltpu.VMEM((slots, LANES), jnp.float32),
        ],
        compiler_params=params(),
    )(embeds, packed, pick)


def ninth_lane(source):
    windows = LANES // CAP
    return CAP * ((source + 1) % windows) + source // windows


def spread_labels(labels, slots):
    row = iota((slots, LANES), 0)
    lane = iota((slots, LANES), 1)
    repeat = ones_where(row // CAP == lane)
    return jnp.where(lane == row % CAP, dot(repeat, labels), 0.0).astype(
        jnp.bfloat16
    )


def fold_block(best, keys, queries, key_labels, query_labels, skip=None):
    same = key_labels == query_labels
    if skip is not None:
        same = same & ~skip
    return jnp.maximum(
        best, jnp.max(jnp.where(same, dot_t(keys, queries), -1.0), axis=0, keepdims=True)
    )


def own_kernel(rows_ref, best_ref, labels_ref, last_ref, ninth_ref, column_ref):
    slots, wide = rows_ref.shape
    width = wide - LANES
    sources = slots // CAP
    last_ref[...] = rows_ref[:, width:].astype(jnp.float32)
    for piece in range(width // LANES):
        ninth_ref[:, piece * LANES : (piece + 1) * LANES] = last_ref[
            pl.ds(piece, sources, stride=CAP), :
        ].astype(jnp.bfloat16)
    labels = last_ref[pl.ds(width // LANES, sources, stride=CAP), :].astype(jnp.bfloat16)
    spots = spread_labels(labels, slots)
    order = ones_where(iota((sources, LANES), 0) == ninth_lane(iota((sources, LANES), 1)))
    ninth_ref[...] = dot(order, ninth_ref[...]).astype(jnp.bfloat16)
    labels = dot(order, labels).astype(jnp.bfloat16)
    ones = jnp.ones((LANES, LANES), jnp.bfloat16)
    column_ref[:slots, :] = dot(spots, ones)
    at_ninth = ones_where(iota((LANES, LANES), 0) == CAP)
    column_ref[slots:, :] = dot(labels, at_ninth)
    at_ninth = ones_where(iota((CAP, LANES), 1) == CAP)
    row_labels = jnp.concatenate(
        [dot_t(ones[:CAP], spots), dot_t(at_ninth, labels)], axis=1
    )
    labels_ref[...] = row_labels

    block = 256
    starts = list(range(0, slots, block)) + [slots]
    sizes = [block] * (slots // block) + [sources]

    def read(i):
        if starts[i] == slots:
            return ninth_ref[...]
        return rows_ref[starts[i] : starts[i] + block, :width]

    for q, (query, size) in enumerate(zip(starts, sizes)):
        best = jnp.full((1, size), -1.0, jnp.float32)
        queries = read(q)
        for k, (key, count) in enumerate(zip(starts, sizes)):
            skip = None
            if k == q:
                skip = iota((count, size), 0) == iota((count, size), 1)
            best = fold_block(
                best,
                read(k),
                queries,
                column_ref[key : key + count, :1],
                row_labels[:1, query : query + size],
                skip,
            )
        best_ref[:, query : query + size] = best


def own_best(arrived):
    slots, wide = arrived.shape
    count = slots + slots // CAP
    return pl.pallas_call(
        own_kernel,
        out_shape=(
            jax.ShapeDtypeStruct((1, count), jnp.float32),
            jax.ShapeDtypeStruct((CAP, count), jnp.float32),
        ),
        scratch_shapes=[
            pltpu.VMEM((slots, LANES), jnp.float32),
            pltpu.VMEM((slots // CAP, wide - LANES), jnp.bfloat16),
            pltpu.VMEM((count, LANES), jnp.float32),
        ],
        compiler_params=params(),
    )(arrived)


def cross_kernel(best_ref, labels_ref, rows_ref, other_ref, out_ref, last_ref, column_ref):
    slots, wide = rows_ref.shape
    width = wide - LANES
    sources = slots // CAP
    last_ref[...] = other_ref[:, width:].astype(jnp.float32)
    labels = last_ref[pl.ds(width // LANES, sources, stride=CAP), :].astype(jnp.bfloat16)
    column_ref[...] = dot(
        spread_labels(labels, slots), jnp.ones((LANES, LANES), jnp.bfloat16)
    )
    block = 256

    def run(last_key, first_query):
        own = [best_ref[:, q : q + block] for q in range(0, slots, block)]
        gained = [jnp.full((1, LANES), -1.0, jnp.float32)] * (slots // LANES)
        for k in range(0, last_key, block):
            widest = jnp.full((block, LANES), -1.0, jnp.float32)
            for q in range(first_query, slots, block):
                scores = dot_t(other_ref[k : k + block, :width], rows_ref[q : q + block, :width])
                same = column_ref[k : k + block, :1] == labels_ref[:1, q : q + block]
                scores = jnp.where(same, scores, -1.0)
                own[q // block] = jnp.maximum(
                    own[q // block], jnp.max(scores, axis=0, keepdims=True)
                )
                for lane in range(0, block, LANES):
                    widest = jnp.maximum(widest, scores[:, lane : lane + LANES])
            for j in range(0, block, LANES):
                gained[(k + j) // LANES] = jnp.max(
                    widest[j : j + LANES].T, axis=0, keepdims=True
                )
        windows = LANES // CAP
        own = jnp.concatenate(own, axis=1)
        tiles = range(slots // LANES)
        own = jnp.concatenate(
            [
                jnp.broadcast_to(own[:, t * LANES : (t + 1) * LANES], (windows, LANES))
                for t in tiles
            ],
            axis=0,
        )
        gained = jnp.concatenate(
            [jnp.broadcast_to(gained[t], (windows, LANES)) for t in tiles], axis=0
        )
        gained = pltpu.roll(gained, LANES // 2, 1)
        ninth = jnp.broadcast_to(best_ref[:, slots:], (sources, LANES))
        window = iota((sources, LANES), 1) // CAP
        mine = iota((sources, LANES), 0) % windows
        out_ref[...] = jnp.where(
            window == mine,
            own,
            jnp.where(window == (mine + windows // 2) % windows, gained, ninth),
        )

    core = lax.axis_index("mem") % 2

    @pl.when(core == 0)
    def _():
        run(slots // 2, 0)

    @pl.when(core == 1)
    def _():
        run(slots, slots // 2)


def cross_best(best, labels, arrived, other):
    slots = arrived.shape[0]
    return pl.pallas_call(
        cross_kernel,
        out_shape=jax.ShapeDtypeStruct((slots // CAP, LANES), jnp.float32),
        scratch_shapes=[
            pltpu.VMEM((slots, LANES), jnp.float32),
            pltpu.VMEM((slots, LANES), jnp.float32),
        ],
        compiler_params=params(),
    )(best, labels, arrived, other)


def lookup_kernel(members, table_ref, dest_ref, out_ref):
    devices = table_ref.shape[0]
    rows = dest_ref.shape[1]
    windows = LANES // CAP
    me = lax.axis_index("grp") * members + lax.axis_index("mem")
    mine = me % windows
    table = table_ref[...]
    turned = pltpu.roll(table, LANES // 2, 1)
    even = iota((devices, LANES), 0) % 2 == 0
    other = jnp.where(even, pltpu.roll(turned, devices - 1, 0), pltpu.roll(turned, 1, 0))
    window = iota((devices, LANES), 1) // CAP
    table = jnp.where(window == mine, jnp.maximum(table, other), table)
    device, row = place(dest_ref[...], members)
    pick = jnp.where(iota((devices, rows), 0) == device, 1.0, 0.0)
    found = lax.dot_general(
        table, pick, (((0,), (0,)), ((), ())), precision=HIGHEST,
        preferred_element_type=jnp.float32,
    )
    lane = jnp.where(row < CAP, CAP * mine + row, ninth_lane(me))
    out_ref[...] = jnp.max(
        jnp.where(iota((LANES, rows), 0) == lane, found, -1.0), axis=0, keepdims=True
    )


def lookup(table, dest, members):
    rows = dest.shape[0]
    return pl.pallas_call(
        functools.partial(lookup_kernel, members),
        out_shape=jax.ShapeDtypeStruct((1, rows), jnp.float32),
        compiler_params=params(),
    )(table, dest.reshape(1, rows)).reshape(rows)


def shards(embeds, cluster, dest):
    members = lax.axis_size("mem")
    devices = lax.axis_size("grp") * members
    width = embeds.shape[1]
    slots = devices * CAP
    outgoing = pack(embeds, cluster, dest, slots, members)
    arrived = lax.all_to_all(
        outgoing.reshape(devices, CAP, width + LANES),
        ("grp", "mem"),
        split_axis=0,
        concat_axis=0,
        tiled=True,
    ).reshape(slots, width + LANES)
    other = lax.ppermute(arrived, "mem", [(m, m ^ 1) for m in range(members)])
    best, labels = own_best(arrived)
    table = cross_best(best, labels, arrived, other)
    returned = lax.all_to_all(
        table.reshape(devices, 1, LANES),
        ("grp", "mem"),
        split_axis=0,
        concat_axis=0,
        tiled=True,
    ).reshape(devices, LANES)
    return lookup(returned, dest, members)


def solution(mesh):
    placed = (P(("grp", "mem"), None), P(("grp", "mem")), P(("grp", "mem")))
    return jax.shard_map(
        shards, mesh=mesh, in_specs=placed, out_specs=P(("grp", "mem")), check_vma=False
    )
```

```python
import functools

import jax
import jax.numpy as jnp
from jax import lax
from jax.experimental import pallas as pl
from jax.experimental.pallas import tpu as pltpu
from jax.sharding import PartitionSpec as P

CAP = 8
SHARED = 2
KEPT = CAP - SHARED
SPLIT = KEPT // 2
LANES = 128
VMEM_LIMIT = 48 * 1024 * 1024


def place(dest, members):
    owner = dest // CAP
    group = owner // members
    member = owner % members
    column = dest % CAP
    shared = member * SHARED + column
    index = column - SHARED
    third = member % 3
    halved = third == 2
    spread = column < SHARED
    core = jnp.where(
        spread, shared // CAP, jnp.where(halved, index // SPLIT, third)
    )
    chip = jnp.where(spread, members // 2 - 1, (1 + member // 3) % 3)
    row = jnp.where(
        spread, shared % CAP, jnp.where(halved, index % SPLIT, index + SPLIT)
    )
    return group * members + 2 * chip + core, row


def params():
    return pltpu.CompilerParams(vmem_limit_bytes=VMEM_LIMIT)


def iota(shape, axis):
    return lax.broadcasted_iota(jnp.int32, shape, axis)


def dot(a, b):
    return jnp.dot(a, b, preferred_element_type=jnp.float32)


def dot_t(a, b):
    return lax.dot_general(a, b, (((1,), (1,)), ((), ())), preferred_element_type=jnp.float32)


def ones_where(mask):
    return jnp.where(mask, 1.0, 0.0).astype(jnp.bfloat16)


def pack_kernel(embeds_ref, packed_ref, pick_ref, out_ref, unit_ref, last_ref):
    rows, width = embeds_ref.shape
    slots = out_ref.shape[0]
    devices = slots // CAP
    packed = packed_ref[...]
    spot = packed % (2 * slots)
    label = (packed // (2 * slots)).astype(jnp.float32)
    device = jnp.where(spot < slots, spot // CAP, spot - slots)
    row = jnp.where(spot < slots, spot % CAP, CAP)

    values = embeds_ref[...].astype(jnp.float32)
    total = jnp.sum(values * values, axis=1, keepdims=True)
    unit_ref[...] = (values * lax.rsqrt(total + 1e-06)).astype(jnp.bfloat16)

    ninth = dot(pick_ref[slots:, :].astype(jnp.bfloat16), unit_ref[...])
    for piece in range(width // LANES):
        last_ref[pl.ds(piece, devices, stride=CAP), :] = ninth[
            :, piece * LANES : (piece + 1) * LANES
        ]
    here = ones_where(iota((devices, rows), 0) == device)
    marks = jnp.where(iota((LANES, rows), 0) == row, label, 0.0).astype(jnp.bfloat16)
    labels = dot_t(here, marks)
    for piece in range(width // LANES, CAP):
        last_ref[pl.ds(piece, devices, stride=CAP), :] = labels
    out_ref[:, width:] = last_ref[...].astype(jnp.bfloat16)

    block = 256
    for b in range(0, slots, block):
        out_ref[b : b + block, :width] = dot(pick_ref[b : b + block, :].astype(jnp.bfloat16), unit_ref[...]).astype(
            jnp.bfloat16
        )


def pack(embeds, cluster, dest, slots, members):
    rows, width = embeds.shape
    devices = slots // CAP
    device, row = place(dest, members)
    spot = jnp.where(row < CAP, device * CAP + row, slots + device)
    packed = (spot + 2 * slots * (cluster + 1)).reshape(1, rows)
    pick = jnp.where(iota((slots + devices, rows), 0) == spot[None], 1.0, 0.0)
    return pl.pallas_call(
        pack_kernel,
        out_shape=jax.ShapeDtypeStruct((slots, width + LANES), jnp.bfloat16),
        scratch_shapes=[
            pltpu.VMEM((rows, width), jnp.bfloat16),
            pltpu.VMEM((slots, LANES), jnp.float32),
        ],
        compiler_params=params(),
    )(embeds, packed, pick)


def ninth_lane(source):
    windows = LANES // CAP
    return CAP * ((source + 1) % windows) + source // windows


def spread_labels(labels, slots):
    row = iota((slots, LANES), 0)
    lane = iota((slots, LANES), 1)
    repeat = ones_where(row // CAP == lane)
    return jnp.where(lane == row % CAP, dot(repeat, labels), 0.0).astype(
        jnp.bfloat16
    )


def fold_block(best, keys, queries, key_labels, query_labels, skip=None):
    same = key_labels == query_labels
    if skip is not None:
        same = same & ~skip
    return jnp.maximum(
        best, jnp.max(jnp.where(same, dot_t(keys, queries), -1.0), axis=0, keepdims=True)
    )


def own_kernel(rows_ref, best_ref, labels_ref, last_ref, ninth_ref, column_ref):
    slots, wide = rows_ref.shape
    width = wide - LANES
    sources = slots // CAP
    last_ref[...] = rows_ref[:, width:].astype(jnp.float32)
    for piece in range(width // LANES):
        ninth_ref[:, piece * LANES : (piece + 1) * LANES] = last_ref[
            pl.ds(piece, sources, stride=CAP), :
        ].astype(jnp.bfloat16)
    labels = last_ref[pl.ds(width // LANES, sources, stride=CAP), :].astype(jnp.bfloat16)
    spots = spread_labels(labels, slots)
    order = ones_where(iota((sources, LANES), 0) == ninth_lane(iota((sources, LANES), 1)))
    ninth_ref[...] = dot(order, ninth_ref[...]).astype(jnp.bfloat16)
    labels = dot(order, labels).astype(jnp.bfloat16)
    ones = jnp.ones((LANES, LANES), jnp.bfloat16)
    column_ref[:slots, :] = dot(spots, ones)
    at_ninth = ones_where(iota((LANES, LANES), 0) == CAP)
    column_ref[slots:, :] = dot(labels, at_ninth)
    at_ninth = ones_where(iota((CAP, LANES), 1) == CAP)
    row_labels = jnp.concatenate(
        [dot_t(ones[:CAP], spots), dot_t(at_ninth, labels)], axis=1
    )
    labels_ref[...] = row_labels

    block = 256
    starts = list(range(0, slots, block)) + [slots]
    sizes = [block] * (slots // block) + [sources]

    def read(i):
        if starts[i] == slots:
            return ninth_ref[...]
        return rows_ref[starts[i] : starts[i] + block, :width]

    for q, (query, size) in enumerate(zip(starts, sizes)):
        best = jnp.full((1, size), -1.0, jnp.float32)
        queries = read(q)
        for k, (key, count) in enumerate(zip(starts, sizes)):
            skip = None
            if k == q:
                skip = iota((count, size), 0) == iota((count, size), 1)
            best = fold_block(
                best,
                read(k),
                queries,
                column_ref[key : key + count, :1],
                row_labels[:1, query : query + size],
                skip,
            )
        best_ref[:, query : query + size] = best


def own_best(arrived):
    slots, wide = arrived.shape
    count = slots + slots // CAP
    return pl.pallas_call(
        own_kernel,
        out_shape=(
            jax.ShapeDtypeStruct((1, count), jnp.float32),
            jax.ShapeDtypeStruct((CAP, count), jnp.float32),
        ),
        scratch_shapes=[
            pltpu.VMEM((slots, LANES), jnp.float32),
            pltpu.VMEM((slots // CAP, wide - LANES), jnp.bfloat16),
            pltpu.VMEM((count, LANES), jnp.float32),
        ],
        compiler_params=params(),
    )(arrived)


def cross_kernel(best_ref, labels_ref, rows_ref, other_ref, out_ref, last_ref, column_ref):
    slots, wide = rows_ref.shape
    width = wide - LANES
    sources = slots // CAP
    block = 256

    def run(last_key, first_query):
        if last_key:
            last_ref[...] = other_ref[:, width:].astype(jnp.float32)
            labels = last_ref[pl.ds(width // LANES, sources, stride=CAP), :].astype(jnp.bfloat16)
            column_ref[...] = dot(
                spread_labels(labels, slots), jnp.ones((LANES, LANES), jnp.bfloat16)
            )
        own = [best_ref[:, q : q + block] for q in range(0, slots, block)]
        gained = [jnp.full((1, LANES), -1.0, jnp.float32)] * (slots // LANES)
        for k in range(0, last_key, block):
            widest = jnp.full((block, LANES), -1.0, jnp.float32)
            for q in range(first_query, slots, block):
                scores = dot_t(other_ref[k : k + block, :width], rows_ref[q : q + block, :width])
                same = column_ref[k : k + block, :1] == labels_ref[:1, q : q + block]
                scores = jnp.where(same, scores, -1.0)
                own[q // block] = jnp.maximum(
                    own[q // block], jnp.max(scores, axis=0, keepdims=True)
                )
                for lane in range(0, block, LANES):
                    widest = jnp.maximum(widest, scores[:, lane : lane + LANES])
            for j in range(0, block, LANES):
                gained[(k + j) // LANES] = jnp.max(
                    widest[j : j + LANES].T, axis=0, keepdims=True
                )
        windows = LANES // CAP
        own = jnp.concatenate(own, axis=1)
        tiles = range(slots // LANES)
        own = jnp.concatenate(
            [
                jnp.broadcast_to(own[:, t * LANES : (t + 1) * LANES], (windows, LANES))
                for t in tiles
            ],
            axis=0,
        )
        gained = jnp.concatenate(
            [jnp.broadcast_to(gained[t], (windows, LANES)) for t in tiles], axis=0
        )
        gained = pltpu.roll(gained, LANES // 2, 1)
        ninth = jnp.broadcast_to(best_ref[:, slots:], (sources, LANES))
        window = iota((sources, LANES), 1) // CAP
        mine = iota((sources, LANES), 0) % windows
        out_ref[...] = jnp.where(
            window == mine,
            own,
            jnp.where(window == (mine + windows // 2) % windows, gained, ninth),
        )

    member = lax.axis_index("mem")
    chip, core = member // 2, member % 2

    @pl.when(chip == 0)
    def _():
        run(0, 0)

    @pl.when((chip > 0) & (core == 0))
    def _():
        run(slots // 2, 0)

    @pl.when((chip > 0) & (core == 1))
    def _():
        run(slots, slots // 2)


def cross_best(best, labels, arrived, other):
    slots = arrived.shape[0]
    return pl.pallas_call(
        cross_kernel,
        out_shape=jax.ShapeDtypeStruct((slots // CAP, LANES), jnp.float32),
        scratch_shapes=[
            pltpu.VMEM((slots, LANES), jnp.float32),
            pltpu.VMEM((slots, LANES), jnp.float32),
        ],
        compiler_params=params(),
    )(best, labels, arrived, other)


def lookup_kernel(members, table_ref, dest_ref, out_ref):
    devices = table_ref.shape[0]
    rows = dest_ref.shape[1]
    windows = LANES // CAP
    me = lax.axis_index("grp") * members + lax.axis_index("mem")
    mine = me % windows
    table = table_ref[...]
    turned = pltpu.roll(table, LANES // 2, 1)
    even = iota((devices, LANES), 0) % 2 == 0
    other = jnp.where(even, pltpu.roll(turned, devices - 1, 0), pltpu.roll(turned, 1, 0))
    window = iota((devices, LANES), 1) // CAP
    table = jnp.where(window == mine, jnp.maximum(table, other), table)
    device, row = place(dest_ref[...], members)
    pick = ones_where(iota((devices, rows), 0) == device)
    parts = []
    left = table.T
    for _ in range(3):
        parts.append(left.astype(jnp.bfloat16))
        left = left - parts[-1].astype(jnp.float32)
    found = dot(jnp.concatenate(parts, axis=1), jnp.concatenate([pick] * 3, axis=0))
    lane = jnp.where(row < CAP, CAP * mine + row, ninth_lane(me))
    out_ref[...] = jnp.max(
        jnp.where(iota((LANES, rows), 0) == lane, found, -1.0), axis=0, keepdims=True
    )


def lookup(table, dest, members):
    rows = dest.shape[0]
    return pl.pallas_call(
        functools.partial(lookup_kernel, members),
        out_shape=jax.ShapeDtypeStruct((1, rows), jnp.float32),
        compiler_params=params(),
    )(table, dest.reshape(1, rows)).reshape(rows)


def shards(embeds, cluster, dest):
    members = lax.axis_size("mem")
    devices = lax.axis_size("grp") * members
    width = embeds.shape[1]
    slots = devices * CAP
    outgoing = pack(embeds, cluster, dest, slots, members)
    arrived = lax.all_to_all(
        outgoing.reshape(devices, CAP, width + LANES),
        ("grp", "mem"),
        split_axis=0,
        concat_axis=0,
        tiled=True,
    ).reshape(slots, width + LANES)
    other = lax.ppermute(arrived, "mem", [(m, m ^ 1) for m in range(members)])
    best, labels = own_best(arrived)
    table = cross_best(best, labels, arrived, other)
    returned = lax.all_to_all(
        table.reshape(devices, 1, LANES),
        ("grp", "mem"),
        split_axis=0,
        concat_axis=0,
        tiled=True,
    ).reshape(devices, LANES)
    return lookup(returned, dest, members)


def solution(mesh):
    placed = (P(("grp", "mem"), None), P(("grp", "mem")), P(("grp", "mem")))
    return jax.shard_map(
        shards, mesh=mesh, in_specs=placed, out_specs=P(("grp", "mem")), check_vma=False
    )
```

```python
import functools

import jax
import jax.numpy as jnp
from jax import lax
from jax.experimental import pallas as pl
from jax.experimental.pallas import tpu as pltpu
from jax.sharding import PartitionSpec as P

CAP = 8
SHARED = 2
KEPT = CAP - SHARED
SPLIT = KEPT // 2
LANES = 128
VMEM_LIMIT = 48 * 1024 * 1024


def place(dest, members):
    owner = dest // CAP
    group = owner // members
    member = owner % members
    column = dest % CAP
    shared = member * SHARED + column
    index = column - SHARED
    third = member % 3
    halved = third == 2
    spread = column < SHARED
    core = jnp.where(
        spread, shared // CAP, jnp.where(halved, index // SPLIT, third)
    )
    chip = jnp.where(spread, 0, 1 + member // 3)
    row = jnp.where(
        spread, shared % CAP, jnp.where(halved, index % SPLIT, index + SPLIT)
    )
    return group, 2 * chip + core, row


def swap_cores(members):
    return [(member, member ^ 1) for member in range(members)]


def params():
    return pltpu.CompilerParams(vmem_limit_bytes=VMEM_LIMIT)


def iota(shape, axis):
    return lax.broadcasted_iota(jnp.int32, shape, axis)


def dot(a, b):
    return jnp.dot(a, b, preferred_element_type=jnp.float32)


def dot_t(a, b):
    return lax.dot_general(a, b, (((1,), (1,)), ((), ())), preferred_element_type=jnp.float32)


def ones_where(mask):
    return jnp.where(mask, 1.0, 0.0).astype(jnp.bfloat16)


def pack_kernel(embeds_ref, packed_ref, pick_ref, out_ref, unit_ref, last_ref):
    rows, width = embeds_ref.shape
    slots = out_ref.shape[0]
    devices = slots // CAP
    packed = packed_ref[...]
    spot = packed % (2 * slots)
    label = (packed // (2 * slots)).astype(jnp.float32)
    device = jnp.where(spot < slots, spot // CAP, spot - slots)
    row = jnp.where(spot < slots, spot % CAP, CAP)

    values = embeds_ref[...].astype(jnp.float32)
    total = jnp.sum(values * values, axis=1, keepdims=True)
    unit_ref[...] = (values * lax.rsqrt(total + 1e-06)).astype(jnp.bfloat16)

    ninth = dot(pick_ref[slots:, :].astype(jnp.bfloat16), unit_ref[...])
    for piece in range(width // LANES):
        last_ref[pl.ds(piece, devices, stride=CAP), :] = ninth[
            :, piece * LANES : (piece + 1) * LANES
        ]
    here = ones_where(iota((devices, rows), 0) == device)
    marks = jnp.where(iota((LANES, rows), 0) == row, label, 0.0).astype(jnp.bfloat16)
    labels = dot_t(here, marks)
    for piece in range(width // LANES, CAP):
        last_ref[pl.ds(piece, devices, stride=CAP), :] = labels
    out_ref[:, width:] = last_ref[...].astype(jnp.bfloat16)

    block = 256
    for b in range(0, slots, block):
        out_ref[b : b + block, :width] = dot(pick_ref[b : b + block, :].astype(jnp.bfloat16), unit_ref[...]).astype(
            jnp.bfloat16
        )


def pack(embeds, cluster, dest, slots, members):
    rows, width = embeds.shape
    devices = slots // CAP
    group, member, row = place(dest, members)
    device = member * (devices // members) + group
    spot = jnp.where(row < CAP, device * CAP + row, slots + device)
    packed = (spot + 2 * slots * (cluster + 1)).reshape(1, rows)
    pick = jnp.where(iota((slots + devices, rows), 0) == spot[None], 1.0, 0.0)
    return pl.pallas_call(
        pack_kernel,
        out_shape=jax.ShapeDtypeStruct((slots, width + LANES), jnp.bfloat16),
        scratch_shapes=[
            pltpu.VMEM((rows, width), jnp.bfloat16),
            pltpu.VMEM((slots, LANES), jnp.float32),
        ],
        compiler_params=params(),
    )(embeds, packed, pick)


def ninth_lane(group, member):
    return CAP * ((group + 1) % (LANES // CAP)) + member


def spread_labels(labels, slots):
    row = iota((slots, LANES), 0)
    lane = iota((slots, LANES), 1)
    repeat = ones_where(iota((slots, len(labels)), 0) // CAP == iota((slots, len(labels)), 1))
    return jnp.where(lane == row % CAP, dot(repeat, labels), 0.0).astype(
        jnp.bfloat16
    )


def widen(widest, scores):
    for lane in range(0, scores.shape[1], LANES):
        widest = jnp.maximum(widest, scores[:, lane : lane + LANES])
    return widest


def across(widest):
    return jnp.concatenate(
        [
            jnp.max(widest[j : j + LANES].T, axis=0, keepdims=True)
            for j in range(0, widest.shape[0], LANES)
        ],
        axis=1,
    )


def own_kernel(rows_ref, best_ref, labels_ref, last_ref, ninth_ref, column_ref):
    slots, wide = rows_ref.shape
    width = wide - LANES
    sources = slots // CAP
    last_ref[...] = rows_ref[:, width:].astype(jnp.float32)
    for piece in range(width // LANES):
        ninth_ref[:, piece * LANES : (piece + 1) * LANES] = last_ref[
            pl.ds(piece, sources, stride=CAP), :
        ].astype(jnp.bfloat16)
    labels = last_ref[pl.ds(width // LANES, sources, stride=CAP), :].astype(jnp.bfloat16)
    spots = spread_labels(labels, slots)
    groups = LANES // CAP
    source = iota((sources, LANES), 1)
    order = ones_where(
        iota((sources, LANES), 0) == ninth_lane(source % groups, source // groups)
    )
    ninth_ref[...] = dot(order, ninth_ref[...]).astype(jnp.bfloat16)
    labels = dot(order, labels).astype(jnp.bfloat16)
    ones = jnp.ones((LANES, LANES), jnp.bfloat16)
    column_ref[:slots, :] = dot(spots, ones)
    at_ninth = ones_where(iota((LANES, LANES), 0) == CAP)
    column_ref[slots:, :] = dot(labels, at_ninth)
    at_ninth = ones_where(iota((CAP, LANES), 1) == CAP)
    row_labels = jnp.concatenate(
        [dot_t(ones[:CAP], spots), dot_t(at_ninth, labels)], axis=1
    )
    labels_ref[...] = row_labels

    block = 256
    starts = list(range(0, slots, block)) + [slots]
    sizes = [block] * (slots // block) + [sources]

    def read(i):
        if starts[i] == slots:
            return ninth_ref[...]
        return rows_ref[starts[i] : starts[i] + block, :width]

    best = [jnp.full((1, size), -1.0, jnp.float32) for size in sizes]
    for k, (key, count) in enumerate(zip(starts, sizes)):
        widest = jnp.full((count, LANES), -1.0, jnp.float32)
        keys = read(k)
        for q in range(k, len(starts)):
            query, size = starts[q], sizes[q]
            scores = dot_t(keys, read(q))
            same = column_ref[key : key + count, :1] == row_labels[:1, query : query + size]
            if q == k:
                same = same & (iota((count, size), 0) != iota((count, size), 1))
            scores = jnp.where(same, scores, -1.0)
            best[q] = jnp.maximum(best[q], jnp.max(scores, axis=0, keepdims=True))
            if q > k:
                widest = widen(widest, scores)
        if k + 1 < len(starts):
            best[k] = jnp.maximum(best[k], across(widest))
        best_ref[:, key : key + count] = best[k]


def own_best(arrived):
    slots, wide = arrived.shape
    count = slots + slots // CAP
    return pl.pallas_call(
        own_kernel,
        out_shape=(
            jax.ShapeDtypeStruct((1, count), jnp.float32),
            jax.ShapeDtypeStruct((CAP, count), jnp.float32),
        ),
        scratch_shapes=[
            pltpu.VMEM((slots, LANES), jnp.float32),
            pltpu.VMEM((slots // CAP, wide - LANES), jnp.bfloat16),
            pltpu.VMEM((count, LANES), jnp.float32),
        ],
        compiler_params=params(),
    )(arrived)


FIRST = ({0: (0, 2, 3), 1: (0, 2, 3)}, {0: (2, 3), 1: (0, 1, 2, 3)})
SECOND = ({2: (2,), 3: (2,)}, {3: (2, 3)})
BLOCKS = 4


def on_each_core(run, plans):
    member = lax.axis_index("mem")
    core = member % 2
    alone = member // 2 == lax.axis_size("mem") // 2 - 1
    pl.when(alone)(lambda: run({}))
    for index, plan in enumerate(plans):
        pl.when(jnp.logical_not(alone) & (core == index))(functools.partial(run, plan))


def meet(plan, best_ref, labels_ref, rows_ref, other_ref, last_ref, column_ref):
    slots, wide = rows_ref.shape
    width = wide - LANES
    block = slots // BLOCKS
    half = other_ref.shape[0]
    if plan:
        last_ref[...] = other_ref[:, width:].astype(jnp.float32)
        labels = last_ref[pl.ds(width // LANES, half // CAP, stride=CAP), :].astype(jnp.bfloat16)
        column_ref[...] = dot(
            spread_labels(labels, half), jnp.ones((LANES, LANES), jnp.bfloat16)
        )
    own = [best_ref[:, q * block : (q + 1) * block] for q in range(BLOCKS)]
    gained = [jnp.full((1, block), -1.0, jnp.float32)] * (BLOCKS // 2)
    for k, queries in plan.items():
        first = k * block % half
        keys = other_ref[first : first + block, :width]
        key_labels = column_ref[first : first + block, :1]
        widest = jnp.full((block, LANES), -1.0, jnp.float32)
        for q in queries:
            scores = dot_t(keys, rows_ref[q * block : (q + 1) * block, :width])
            same = key_labels == labels_ref[:1, q * block : (q + 1) * block]
            scores = jnp.where(same, scores, -1.0)
            own[q] = jnp.maximum(own[q], jnp.max(scores, axis=0, keepdims=True))
            widest = widen(widest, scores)
        gained[k % (BLOCKS // 2)] = across(widest)
    return jnp.concatenate(own, axis=1), jnp.concatenate(gained, axis=1)


def first_kernel(
    best_ref, labels_ref, rows_ref, other_ref, out_ref, gained_ref, last_ref, column_ref
):
    slots = rows_ref.shape[0]

    def run(plan):
        own, gained = meet(
            plan, best_ref, labels_ref, rows_ref, other_ref, last_ref, column_ref
        )
        out_ref[:, :slots] = own
        out_ref[:, slots:] = best_ref[:, slots:]
        gained_ref[...] = gained

    on_each_core(run, FIRST)


def second_kernel(
    best_ref, gained_ref, labels_ref, rows_ref, other_ref, out_ref, last_ref, column_ref
):
    slots = rows_ref.shape[0]
    groups = LANES // CAP
    shape = (groups, LANES)

    def run(plan):
        own, gained = meet(
            plan, best_ref, labels_ref, rows_ref, other_ref, last_ref, column_ref
        )
        gained = jnp.concatenate([gained_ref[...], gained], axis=1)
        window = iota(shape, 1) // CAP
        mine = iota(shape, 0)
        ninth = jnp.broadcast_to(best_ref[:, slots:], shape)
        for first in range(0, slots, LANES):
            tile = slice(first, first + LANES)
            turned = pltpu.roll(jnp.broadcast_to(gained[:, tile], shape), LANES // 2, 1)
            out_ref[first // CAP : first // CAP + groups, :] = jnp.where(
                window == mine,
                jnp.broadcast_to(own[:, tile], shape),
                jnp.where(window == (mine + groups // 2) % groups, turned, ninth),
            )

    on_each_core(run, SECOND)


def cross_best(best, labels, arrived, others):
    slots = arrived.shape[0]
    half = slots // 2
    scratch = [pltpu.VMEM((half, LANES), jnp.float32)] * 2
    best, gained = pl.pallas_call(
        first_kernel,
        out_shape=(
            jax.ShapeDtypeStruct(best.shape, jnp.float32),
            jax.ShapeDtypeStruct((1, half), jnp.float32),
        ),
        scratch_shapes=scratch,
        compiler_params=params(),
    )(best, labels, arrived, others[0])
    return pl.pallas_call(
        second_kernel,
        out_shape=jax.ShapeDtypeStruct((slots // CAP, LANES), jnp.float32),
        scratch_shapes=scratch,
        compiler_params=params(),
    )(best, gained, labels, arrived, others[1])


def lookup_kernel(members, table_ref, dest_ref, out_ref):
    devices = table_ref.shape[0]
    rows = dest_ref.shape[1]
    mine = lax.axis_index("grp")
    groups = devices // members
    table = table_ref[...]
    turned = pltpu.roll(table, LANES // 2, 1)
    core = iota((devices, LANES), 0) // groups % 2
    other = jnp.where(
        core == 0, pltpu.roll(turned, devices - groups, 0), pltpu.roll(turned, groups, 0)
    )
    window = iota((devices, LANES), 1) // CAP
    table = jnp.where(window == mine, jnp.maximum(table, other), table)
    group, member, row = place(dest_ref[...], members)
    pick = ones_where(iota((devices, rows), 0) == member * groups + group)
    parts = []
    left = table.T
    for _ in range(3):
        parts.append(left.astype(jnp.bfloat16))
        left = left - parts[-1].astype(jnp.float32)
    found = dot(jnp.concatenate(parts, axis=1), jnp.concatenate([pick] * 3, axis=0))
    lane = jnp.where(row < CAP, CAP * mine + row, ninth_lane(mine, lax.axis_index("mem")))
    out_ref[...] = jnp.max(
        jnp.where(iota((LANES, rows), 0) == lane, found, -1.0), axis=0, keepdims=True
    )


def lookup(table, dest, members):
    rows = dest.shape[0]
    return pl.pallas_call(
        functools.partial(lookup_kernel, members),
        out_shape=jax.ShapeDtypeStruct((1, rows), jnp.float32),
        compiler_params=params(),
    )(table, dest.reshape(1, rows)).reshape(rows)


def shards(embeds, cluster, dest):
    members = lax.axis_size("mem")
    devices = lax.axis_size("grp") * members
    width = embeds.shape[1]
    slots = devices * CAP
    outgoing = pack(embeds, cluster, dest, slots, members)
    arrived = lax.all_to_all(
        outgoing.reshape(devices, CAP, width + LANES),
        ("mem", "grp"),
        split_axis=0,
        concat_axis=0,
        tiled=True,
    ).reshape(slots, width + LANES)
    half = slots // 2
    others = [
        lax.ppermute(arrived[first : first + half], "mem", swap_cores(members))
        for first in (0, half)
    ]
    best, labels = own_best(arrived)
    table = cross_best(best, labels, arrived, others)
    returned = lax.all_to_all(
        table.reshape(devices, 1, LANES),
        ("mem", "grp"),
        split_axis=0,
        concat_axis=0,
        tiled=True,
    ).reshape(devices, LANES)
    return lookup(returned, dest, members)


def solution(mesh):
    placed = (P(("grp", "mem"), None), P(("grp", "mem")), P(("grp", "mem")))
    return jax.shard_map(
        shards, mesh=mesh, in_specs=placed, out_specs=P(("grp", "mem")), check_vma=False
    )
```

```python
import functools

import jax
import jax.numpy as jnp
from jax import lax
from jax.experimental import pallas as pl
from jax.experimental.pallas import tpu as pltpu
from jax.sharding import PartitionSpec as P

CAP = 8
SHARED = 2
KEPT = CAP - SHARED
SPLIT = KEPT // 2
LANES = 128
VMEM_LIMIT = 48 * 1024 * 1024


def place(dest, members):
    owner = dest // CAP
    group = owner // members
    member = owner % members
    column = dest % CAP
    shared = member * SHARED + column
    index = column - SHARED
    third = member % 3
    halved = third == 2
    spread = column < SHARED
    core = jnp.where(
        spread, shared // CAP, jnp.where(halved, index // SPLIT, third)
    )
    chip = jnp.where(spread, 0, 1 + member // 3)
    row = jnp.where(
        spread, shared % CAP, jnp.where(halved, index % SPLIT, index + SPLIT)
    )
    return group, 2 * chip + core, row


def swap_cores(members):
    return [(member, member ^ 1) for member in range(members)]


def params():
    return pltpu.CompilerParams(vmem_limit_bytes=VMEM_LIMIT)


def iota(shape, axis):
    return lax.broadcasted_iota(jnp.int32, shape, axis)


def dot(a, b):
    return jnp.dot(a, b, preferred_element_type=jnp.float32)


def dot_t(a, b):
    return lax.dot_general(a, b, (((1,), (1,)), ((), ())), preferred_element_type=jnp.float32)


def ones_where(mask):
    return jnp.where(mask, 1.0, 0.0).astype(jnp.bfloat16)


def pack_kernel(
    members, embeds_hbm, cluster_hbm, dest_hbm, out_ref,
    embeds_ref, cluster_ref, dest_ref, unit_ref, last_ref, sems,
):
    rows, width = embeds_ref.shape
    slots = out_ref.shape[0]
    devices = slots // CAP
    block = 256
    copies = [
        pltpu.make_async_copy(source, target, sems.at[index])
        for index, (source, target) in enumerate(
            ((dest_hbm, dest_ref), (cluster_hbm, cluster_ref), (embeds_hbm, embeds_ref))
        )
    ]
    for copy in copies:
        copy.start()
    copies[0].wait()
    copies[1].wait()
    group, member, row = place(dest_ref[...], members)
    device = member * (devices // members) + group
    slot = jnp.where(row < CAP, device * CAP + row, -1)
    picks = [ones_where(b + iota((block, rows), 0) == slot) for b in range(0, slots, block)]
    here = iota((devices, rows), 0) == device
    pick_ninth = ones_where(here & (row == CAP))
    label = (cluster_ref[...] + 1).astype(jnp.float32)
    marks = jnp.where(iota((LANES, rows), 0) == row, label, 0.0).astype(jnp.bfloat16)
    labels = dot_t(ones_where(here), marks)
    for piece in range(width // LANES, CAP):
        last_ref[pl.ds(piece, devices, stride=CAP), :] = labels

    copies[2].wait()
    values = embeds_ref[...].astype(jnp.float32)
    total = jnp.sum(values * values, axis=1, keepdims=True)
    unit_ref[...] = (values * lax.rsqrt(total + 1e-06)).astype(jnp.bfloat16)
    for b, pick in enumerate(picks):
        out_ref[b * block : (b + 1) * block, :width] = dot(pick, unit_ref[...]).astype(
            jnp.bfloat16
        )
    ninth = dot(pick_ninth, unit_ref[...])
    for piece in range(width // LANES):
        last_ref[pl.ds(piece, devices, stride=CAP), :] = ninth[
            :, piece * LANES : (piece + 1) * LANES
        ]
    out_ref[:, width:] = last_ref[...].astype(jnp.bfloat16)


def pack(embeds, cluster, dest, slots, members):
    rows, width = embeds.shape
    operands = [
        pltpu.with_memory_space_constraint(operand, pltpu.HBM)
        for operand in (embeds, cluster.reshape(1, rows), dest.reshape(1, rows))
    ]
    return pl.pallas_call(
        functools.partial(pack_kernel, members),
        out_shape=jax.ShapeDtypeStruct((slots, width + LANES), jnp.bfloat16),
        in_specs=[pl.BlockSpec(memory_space=pltpu.HBM)] * 3,
        scratch_shapes=[
            pltpu.VMEM((rows, width), jnp.bfloat16),
            pltpu.VMEM((1, rows), jnp.int32),
            pltpu.VMEM((1, rows), jnp.int32),
            pltpu.VMEM((rows, width), jnp.bfloat16),
            pltpu.VMEM((slots, LANES), jnp.float32),
            pltpu.SemaphoreType.DMA((3,)),
        ],
        compiler_params=params(),
    )(*operands)


def ninth_lane(group, member):
    return CAP * ((group + 1) % (LANES // CAP)) + member


def spread_labels(labels, slots):
    row = iota((slots, LANES), 0)
    lane = iota((slots, LANES), 1)
    repeat = ones_where(iota((slots, len(labels)), 0) // CAP == iota((slots, len(labels)), 1))
    return jnp.where(lane == row % CAP, dot(repeat, labels), 0.0).astype(
        jnp.bfloat16
    )


def in_every_lane(spots):
    return jnp.broadcast_to(
        jnp.sum(spots.astype(jnp.float32), axis=1, keepdims=True), spots.shape
    )


def masked(scores, key_labels, query_labels, skip=False):
    count, size = scores.shape
    tiles = []
    for lane in range(0, size, LANES):
        same = key_labels == query_labels[:, lane : lane + LANES]
        if skip:
            same = same & (iota((count, LANES), 0) != iota((count, LANES), 1) + lane)
        tiles.append(jnp.where(same, scores[:, lane : lane + LANES], -1.0))
    return jnp.concatenate(tiles, axis=1)


def widen(widest, scores):
    for lane in range(0, scores.shape[1], LANES):
        widest = jnp.maximum(widest, scores[:, lane : lane + LANES])
    return widest


def across(widest):
    return jnp.concatenate(
        [
            jnp.max(widest[j : j + LANES].T, axis=0, keepdims=True)
            for j in range(0, widest.shape[0], LANES)
        ],
        axis=1,
    )


def own_kernel(rows_ref, best_ref, labels_ref, last_ref, ninth_ref, column_ref):
    slots, wide = rows_ref.shape
    width = wide - LANES
    sources = slots // CAP
    last_ref[...] = rows_ref[:, width:].astype(jnp.float32)
    for piece in range(width // LANES):
        ninth_ref[:, piece * LANES : (piece + 1) * LANES] = last_ref[
            pl.ds(piece, sources, stride=CAP), :
        ].astype(jnp.bfloat16)
    labels = last_ref[pl.ds(width // LANES, sources, stride=CAP), :].astype(jnp.bfloat16)
    spots = spread_labels(labels, slots)
    groups = LANES // CAP
    source = iota((sources, LANES), 1)
    order = ones_where(
        iota((sources, LANES), 0) == ninth_lane(source % groups, source // groups)
    )
    ninth_ref[...] = dot(order, ninth_ref[...]).astype(jnp.bfloat16)
    labels = dot(order, labels).astype(jnp.bfloat16)
    ones = jnp.ones((LANES, LANES), jnp.bfloat16)
    column_ref[:slots, :] = in_every_lane(spots)
    at_ninth = ones_where(iota((LANES, LANES), 0) == CAP)
    column_ref[slots:, :] = dot(labels, at_ninth)
    at_ninth = ones_where(iota((CAP, LANES), 1) == CAP)
    row_labels = jnp.concatenate(
        [dot_t(ones[:CAP], spots), dot_t(at_ninth, labels)], axis=1
    )
    labels_ref[...] = row_labels

    block = 256
    starts = list(range(0, slots, block)) + [slots]
    sizes = [block] * (slots // block) + [sources]

    def read(i):
        if starts[i] == slots:
            return ninth_ref[...]
        return rows_ref[starts[i] : starts[i] + block, :width]

    best = [jnp.full((1, size), -1.0, jnp.float32) for size in sizes]
    for k, (key, count) in enumerate(zip(starts, sizes)):
        widest = jnp.full((count, LANES), -1.0, jnp.float32)
        keys = read(k)
        for q in range(k, len(starts)):
            query, size = starts[q], sizes[q]
            scores = masked(
                dot_t(keys, read(q)),
                column_ref[key : key + count, :],
                row_labels[:1, query : query + size],
                q == k,
            )
            best[q] = jnp.maximum(best[q], jnp.max(scores, axis=0, keepdims=True))
            if q > k:
                widest = widen(widest, scores)
        if k + 1 < len(starts):
            best[k] = jnp.maximum(best[k], across(widest))
        best_ref[:, key : key + count] = best[k]


def own_best(arrived):
    slots, wide = arrived.shape
    count = slots + slots // CAP
    return pl.pallas_call(
        own_kernel,
        out_shape=(
            jax.ShapeDtypeStruct((1, count), jnp.float32),
            jax.ShapeDtypeStruct((CAP, count), jnp.float32),
        ),
        scratch_shapes=[
            pltpu.VMEM((slots, LANES), jnp.float32),
            pltpu.VMEM((slots // CAP, wide - LANES), jnp.bfloat16),
            pltpu.VMEM((count, LANES), jnp.float32),
        ],
        compiler_params=params(),
    )(arrived)


FIRST = ({0: (0, 2, 3), 1: (0, 2, 3)}, {0: (2, 3), 1: (0, 1, 2, 3)})
SECOND = ({2: (2,), 3: (2,)}, {3: (2, 3)})
BLOCKS = 4


def on_each_core(run, plans):
    member = lax.axis_index("mem")
    core = member % 2
    alone = member // 2 == lax.axis_size("mem") // 2 - 1
    pl.when(alone)(lambda: run({}))
    for index, plan in enumerate(plans):
        pl.when(jnp.logical_not(alone) & (core == index))(functools.partial(run, plan))


def meet(plan, best_ref, labels_ref, rows_ref, other_ref, last_ref, column_ref):
    slots, wide = rows_ref.shape
    width = wide - LANES
    block = slots // BLOCKS
    half = other_ref.shape[0]
    if plan:
        last_ref[...] = other_ref[:, width:].astype(jnp.float32)
        labels = last_ref[pl.ds(width // LANES, half // CAP, stride=CAP), :].astype(jnp.bfloat16)
        column_ref[...] = in_every_lane(spread_labels(labels, half))
    own = [best_ref[:, q * block : (q + 1) * block] for q in range(BLOCKS)]
    gained = [jnp.full((1, block), -1.0, jnp.float32)] * (BLOCKS // 2)
    for k, queries in plan.items():
        first = k * block % half
        keys = other_ref[first : first + block, :width]
        key_labels = column_ref[first : first + block, :]
        widest = jnp.full((block, LANES), -1.0, jnp.float32)
        for q in queries:
            scores = masked(
                dot_t(keys, rows_ref[q * block : (q + 1) * block, :width]),
                key_labels,
                labels_ref[:1, q * block : (q + 1) * block],
            )
            own[q] = jnp.maximum(own[q], jnp.max(scores, axis=0, keepdims=True))
            widest = widen(widest, scores)
        gained[k % (BLOCKS // 2)] = across(widest)
    return jnp.concatenate(own, axis=1), jnp.concatenate(gained, axis=1)


def first_kernel(
    best_ref, labels_ref, rows_ref, other_ref, out_ref, gained_ref, last_ref, column_ref
):
    slots = rows_ref.shape[0]

    def run(plan):
        own, gained = meet(
            plan, best_ref, labels_ref, rows_ref, other_ref, last_ref, column_ref
        )
        out_ref[:, :slots] = own
        out_ref[:, slots:] = best_ref[:, slots:]
        gained_ref[...] = gained

    on_each_core(run, FIRST)


def second_kernel(
    best_ref, gained_ref, labels_ref, rows_ref, other_ref, out_ref, last_ref, column_ref
):
    slots = rows_ref.shape[0]
    groups = LANES // CAP
    shape = (groups, LANES)

    def run(plan):
        own, gained = meet(
            plan, best_ref, labels_ref, rows_ref, other_ref, last_ref, column_ref
        )
        gained = jnp.concatenate([gained_ref[...], gained], axis=1)
        window = iota(shape, 1) // CAP
        mine = iota(shape, 0)
        ninth = jnp.broadcast_to(best_ref[:, slots:], shape)
        for first in range(0, slots, LANES):
            tile = slice(first, first + LANES)
            turned = pltpu.roll(jnp.broadcast_to(gained[:, tile], shape), LANES // 2, 1)
            out_ref[first // CAP : first // CAP + groups, :] = jnp.where(
                window == mine,
                jnp.broadcast_to(own[:, tile], shape),
                jnp.where(window == (mine + groups // 2) % groups, turned, ninth),
            )

    on_each_core(run, SECOND)


def cross_best(best, labels, arrived, others):
    slots = arrived.shape[0]
    half = slots // 2
    scratch = [pltpu.VMEM((half, LANES), jnp.float32)] * 2
    best, gained = pl.pallas_call(
        first_kernel,
        out_shape=(
            jax.ShapeDtypeStruct(best.shape, jnp.float32),
            jax.ShapeDtypeStruct((1, half), jnp.float32),
        ),
        scratch_shapes=scratch,
        compiler_params=params(),
    )(best, labels, arrived, others[0])
    return pl.pallas_call(
        second_kernel,
        out_shape=jax.ShapeDtypeStruct((slots // CAP, LANES), jnp.float32),
        scratch_shapes=scratch,
        compiler_params=params(),
    )(best, gained, labels, arrived, others[1])


def lookup_kernel(members, table_ref, dest_ref, out_ref):
    devices = table_ref.shape[0]
    rows = dest_ref.shape[1]
    mine = lax.axis_index("grp")
    groups = devices // members
    table = table_ref[...]
    turned = pltpu.roll(table, LANES // 2, 1)
    core = iota((devices, LANES), 0) // groups % 2
    other = jnp.where(
        core == 0, pltpu.roll(turned, devices - groups, 0), pltpu.roll(turned, groups, 0)
    )
    window = iota((devices, LANES), 1) // CAP
    table = jnp.where(window == mine, jnp.maximum(table, other), table)
    group, member, row = place(dest_ref[...], members)
    pick = ones_where(iota((devices, rows), 0) == member * groups + group)
    parts = []
    left = table.T
    for _ in range(3):
        parts.append(left.astype(jnp.bfloat16))
        left = left - parts[-1].astype(jnp.float32)
    found = dot(jnp.concatenate(parts, axis=1), jnp.concatenate([pick] * 3, axis=0))
    lane = jnp.where(row < CAP, CAP * mine + row, ninth_lane(mine, lax.axis_index("mem")))
    out_ref[...] = jnp.max(
        jnp.where(iota((LANES, rows), 0) == lane, found, -1.0), axis=0, keepdims=True
    )


def lookup(table, dest, members):
    rows = dest.shape[0]
    return pl.pallas_call(
        functools.partial(lookup_kernel, members),
        out_shape=jax.ShapeDtypeStruct((1, rows), jnp.float32),
        compiler_params=params(),
    )(table, dest.reshape(1, rows)).reshape(rows)


def shards(embeds, cluster, dest):
    members = lax.axis_size("mem")
    devices = lax.axis_size("grp") * members
    width = embeds.shape[1]
    slots = devices * CAP
    outgoing = pack(embeds, cluster, dest, slots, members)
    arrived = lax.all_to_all(
        outgoing.reshape(devices, CAP, width + LANES),
        ("mem", "grp"),
        split_axis=0,
        concat_axis=0,
        tiled=True,
    ).reshape(slots, width + LANES)
    half = slots // 2
    others = [
        lax.ppermute(arrived[first : first + half], "mem", swap_cores(members))
        for first in (0, half)
    ]
    best, labels = own_best(arrived)
    table = cross_best(best, labels, arrived, others)
    returned = lax.all_to_all(
        table.reshape(devices, 1, LANES),
        ("mem", "grp"),
        split_axis=0,
        concat_axis=0,
        tiled=True,
    ).reshape(devices, LANES)
    return lookup(returned, dest, members)


def solution(mesh):
    placed = (P(("grp", "mem"), None), P(("grp", "mem")), P(("grp", "mem")))
    return jax.shard_map(
        shards, mesh=mesh, in_specs=placed, out_specs=P(("grp", "mem")), check_vma=False
    )
```

```python
import functools

import jax
import jax.numpy as jnp
from jax import lax
from jax.experimental import pallas as pl
from jax.experimental.pallas import tpu as pltpu
from jax.sharding import PartitionSpec as P

CAP = 8
SHARED = 2
KEPT = CAP - SHARED
SPLIT = KEPT // 2
LANES = 128
OTHERS = 2 * CAP
VMEM_LIMIT = 48 * 1024 * 1024


def place(dest, members):
    owner = dest // CAP
    group = owner // members
    member = owner % members
    column = dest % CAP
    shared = member * SHARED + column
    index = column - SHARED
    third = member % 3
    halved = third == 2
    spread = column < SHARED
    core = jnp.where(
        spread, shared // CAP, jnp.where(halved, index // SPLIT, third)
    )
    chip = jnp.where(spread, 0, 1 + member // 3)
    row = jnp.where(
        spread, shared % CAP, jnp.where(halved, index % SPLIT, index + SPLIT)
    )
    return group, 2 * chip + core, row


def swap_cores(members):
    return [(member, member ^ 1) for member in range(members)]


def params():
    return pltpu.CompilerParams(vmem_limit_bytes=VMEM_LIMIT)


def iota(shape, axis):
    return lax.broadcasted_iota(jnp.int32, shape, axis)


def dot(a, b):
    return jnp.dot(a, b, preferred_element_type=jnp.float32)


def dot_t(a, b):
    return lax.dot_general(a, b, (((1,), (1,)), ((), ())), preferred_element_type=jnp.float32)


def ones_where(mask):
    return jnp.where(mask, 1.0, 0.0).astype(jnp.bfloat16)


def label_lines(lane, label):
    return jnp.where(iota((LANES, lane.shape[1]), 0) == lane, label, 0.0).astype(jnp.bfloat16)


def pack_kernel(
    members, embeds_hbm, cluster_hbm, dest_hbm, out_ref,
    embeds_ref, cluster_ref, dest_ref, unit_ref, last_ref, sems,
):
    rows, width = embeds_ref.shape
    slots = out_ref.shape[0]
    devices = slots // CAP
    block = 256
    copies = [
        pltpu.make_async_copy(source, target, sems.at[index])
        for index, (source, target) in enumerate(
            ((dest_hbm, dest_ref), (cluster_hbm, cluster_ref), (embeds_hbm, embeds_ref))
        )
    ]
    for copy in copies:
        copy.start()
    copies[0].wait()
    copies[1].wait()
    group, member, row = place(dest_ref[...], members)
    device = member * (devices // members) + group
    slot = jnp.where(row < CAP, device * CAP + row, -1)
    picks = [ones_where(b + iota((block, rows), 0) == slot) for b in range(0, slots, block)]
    here = iota((devices, rows), 0) == device
    pick_ninth = ones_where(here & (row == CAP))
    label = (cluster_ref[...] + 1).astype(jnp.float32)
    labels = dot_t(ones_where(here), label_lines(row, label))
    other = (member ^ 1) * (devices // members) + group
    here_other = ones_where(iota((devices, rows), 0) == other)
    labels += dot_t(here_other, label_lines(row + OTHERS, label))
    for piece in range(width // LANES, CAP):
        last_ref[pl.ds(piece, devices, stride=CAP), :] = labels

    copies[2].wait()
    values = embeds_ref[...].astype(jnp.float32)
    total = jnp.sum(values * values, axis=1, keepdims=True)
    unit_ref[...] = (values * lax.rsqrt(total + 1e-06)).astype(jnp.bfloat16)
    for b, pick in enumerate(picks):
        out_ref[b * block : (b + 1) * block, :width] = dot(pick, unit_ref[...]).astype(
            jnp.bfloat16
        )
    ninth = dot(pick_ninth, unit_ref[...])
    for piece in range(width // LANES):
        last_ref[pl.ds(piece, devices, stride=CAP), :] = ninth[
            :, piece * LANES : (piece + 1) * LANES
        ]
    out_ref[:, width:] = last_ref[...].astype(jnp.bfloat16)


def pack(embeds, cluster, dest, slots, members):
    rows, width = embeds.shape
    operands = [
        pltpu.with_memory_space_constraint(operand, pltpu.HBM)
        for operand in (embeds, cluster.reshape(1, rows), dest.reshape(1, rows))
    ]
    return pl.pallas_call(
        functools.partial(pack_kernel, members),
        out_shape=jax.ShapeDtypeStruct((slots, width + LANES), jnp.bfloat16),
        in_specs=[pl.BlockSpec(memory_space=pltpu.HBM)] * 3,
        scratch_shapes=[
            pltpu.VMEM((rows, width), jnp.bfloat16),
            pltpu.VMEM((1, rows), jnp.int32),
            pltpu.VMEM((1, rows), jnp.int32),
            pltpu.VMEM((rows, width), jnp.bfloat16),
            pltpu.VMEM((slots, LANES), jnp.float32),
            pltpu.SemaphoreType.DMA((3,)),
        ],
        compiler_params=params(),
    )(*operands)


def ninth_lane(group, member):
    return CAP * ((group + 1) % (LANES // CAP)) + member


def repeat_lines(labels, slots):
    shape = (slots, labels.shape[0])
    return dot(ones_where(iota(shape, 0) // CAP == iota(shape, 1)), labels)


def only_own(lines, first):
    own = iota(lines.shape, 1) == first + iota(lines.shape, 0) % CAP
    return jnp.where(own, lines, 0.0)


def in_every_lane(spots):
    return jnp.broadcast_to(jnp.sum(spots, axis=1, keepdims=True), spots.shape)


def masked(scores, key_labels, query_labels, skip=False):
    count, size = scores.shape
    tiles = []
    for lane in range(0, size, LANES):
        same = key_labels == query_labels[:, lane : lane + LANES]
        if skip:
            same = same & (iota((count, LANES), 0) != iota((count, LANES), 1) + lane)
        tiles.append(jnp.where(same, scores[:, lane : lane + LANES], -1.0))
    return jnp.concatenate(tiles, axis=1)


def widen(widest, scores):
    for lane in range(0, scores.shape[1], LANES):
        widest = jnp.maximum(widest, scores[:, lane : lane + LANES])
    return widest


def across(widest):
    return jnp.concatenate(
        [
            jnp.max(widest[j : j + LANES].T, axis=0, keepdims=True)
            for j in range(0, widest.shape[0], LANES)
        ],
        axis=1,
    )


def own_kernel(
    rows_ref, best_ref, labels_ref, others_ref, last_ref, ninth_ref, column_ref
):
    slots, wide = rows_ref.shape
    width = wide - LANES
    sources = slots // CAP
    last_ref[...] = rows_ref[:, width:].astype(jnp.float32)
    for piece in range(width // LANES):
        ninth_ref[:, piece * LANES : (piece + 1) * LANES] = last_ref[
            pl.ds(piece, sources, stride=CAP), :
        ].astype(jnp.bfloat16)
    labels = last_ref[pl.ds(width // LANES, sources, stride=CAP), :].astype(jnp.bfloat16)
    lines = repeat_lines(labels, slots)
    spots = only_own(lines, 0)
    others_ref[...] = in_every_lane(only_own(lines, OTHERS))
    groups = LANES // CAP
    source = iota((sources, LANES), 1)
    order = ones_where(
        iota((sources, LANES), 0) == ninth_lane(source % groups, source // groups)
    )
    ninth_ref[...] = dot(order, ninth_ref[...]).astype(jnp.bfloat16)
    labels = dot(order, labels).astype(jnp.bfloat16)
    ones = jnp.ones((LANES, LANES), jnp.bfloat16)
    column_ref[:slots, :] = in_every_lane(spots)
    at_ninth = ones_where(iota((LANES, LANES), 0) == CAP)
    column_ref[slots:, :] = dot(labels, at_ninth)
    at_ninth = ones_where(iota((CAP, LANES), 1) == CAP)
    row_labels = jnp.concatenate(
        [dot_t(ones[:CAP], spots.astype(jnp.bfloat16)), dot_t(at_ninth, labels)], axis=1
    )
    labels_ref[...] = row_labels

    block = 256
    starts = list(range(0, slots, block)) + [slots]
    sizes = [block] * (slots // block) + [sources]

    def read(i):
        if starts[i] == slots:
            return ninth_ref[...]
        return rows_ref[starts[i] : starts[i] + block, :width]

    best = [jnp.full((1, size), -1.0, jnp.float32) for size in sizes]
    for k, (key, count) in enumerate(zip(starts, sizes)):
        widest = jnp.full((count, LANES), -1.0, jnp.float32)
        keys = read(k)
        for q in range(k, len(starts)):
            query, size = starts[q], sizes[q]
            scores = masked(
                dot_t(keys, read(q)),
                column_ref[key : key + count, :],
                row_labels[:1, query : query + size],
                q == k,
            )
            best[q] = jnp.maximum(best[q], jnp.max(scores, axis=0, keepdims=True))
            if q > k:
                widest = widen(widest, scores)
        if k + 1 < len(starts):
            best[k] = jnp.maximum(best[k], across(widest))
        best_ref[:, key : key + count] = best[k]


def own_best(arrived):
    slots, wide = arrived.shape
    count = slots + slots // CAP
    return pl.pallas_call(
        own_kernel,
        out_shape=(
            jax.ShapeDtypeStruct((1, count), jnp.float32),
            jax.ShapeDtypeStruct((CAP, count), jnp.float32),
            jax.ShapeDtypeStruct((slots, LANES), jnp.float32),
        ),
        scratch_shapes=[
            pltpu.VMEM((slots, LANES), jnp.float32),
            pltpu.VMEM((slots // CAP, wide - LANES), jnp.bfloat16),
            pltpu.VMEM((count, LANES), jnp.float32),
        ],
        compiler_params=params(),
    )(arrived)


FIRST = ({0: (0, 2, 3), 1: (0, 2, 3)}, {0: (2, 3), 1: (0, 1, 2, 3)})
SECOND = ({2: (2,), 3: (2,)}, {3: (2, 3)})
BLOCKS = 4


def on_each_core(run, plans):
    member = lax.axis_index("mem")
    core = member % 2
    alone = member // 2 == lax.axis_size("mem") // 2 - 1
    pl.when(alone)(lambda: run({}))
    for index, plan in enumerate(plans):
        pl.when(jnp.logical_not(alone) & (core == index))(functools.partial(run, plan))


def meet(plan, best_ref, labels_ref, others_ref, rows_ref, other_ref):
    slots = rows_ref.shape[0]
    half, width = other_ref.shape
    block = slots // BLOCKS
    own = [best_ref[:, q * block : (q + 1) * block] for q in range(BLOCKS)]
    gained = [jnp.full((1, block), -1.0, jnp.float32)] * (BLOCKS // 2)
    for k, queries in plan.items():
        first = k * block % half
        keys = other_ref[first : first + block, :]
        key_labels = others_ref[k * block : (k + 1) * block, :]
        widest = jnp.full((block, LANES), -1.0, jnp.float32)
        for q in queries:
            scores = masked(
                dot_t(keys, rows_ref[q * block : (q + 1) * block, :width]),
                key_labels,
                labels_ref[:1, q * block : (q + 1) * block],
            )
            own[q] = jnp.maximum(own[q], jnp.max(scores, axis=0, keepdims=True))
            widest = widen(widest, scores)
        gained[k % (BLOCKS // 2)] = across(widest)
    return jnp.concatenate(own, axis=1), jnp.concatenate(gained, axis=1)


def first_kernel(
    best_ref, labels_ref, others_ref, rows_ref, other_ref, out_ref, gained_ref
):
    slots = rows_ref.shape[0]

    def run(plan):
        own, gained = meet(plan, best_ref, labels_ref, others_ref, rows_ref, other_ref)
        out_ref[:, :slots] = own
        out_ref[:, slots:] = best_ref[:, slots:]
        gained_ref[...] = gained

    on_each_core(run, FIRST)


def second_kernel(
    best_ref, gained_ref, labels_ref, others_ref, rows_ref, other_ref, out_ref
):
    slots = rows_ref.shape[0]
    groups = LANES // CAP
    shape = (groups, LANES)

    def run(plan):
        own, gained = meet(plan, best_ref, labels_ref, others_ref, rows_ref, other_ref)
        gained = jnp.concatenate([gained_ref[...], gained], axis=1)
        window = iota(shape, 1) // CAP
        mine = iota(shape, 0)
        ninth = jnp.broadcast_to(best_ref[:, slots:], shape)
        for first in range(0, slots, LANES):
            tile = slice(first, first + LANES)
            turned = pltpu.roll(jnp.broadcast_to(gained[:, tile], shape), LANES // 2, 1)
            out_ref[first // CAP : first // CAP + groups, :] = jnp.where(
                window == mine,
                jnp.broadcast_to(own[:, tile], shape),
                jnp.where(window == (mine + groups // 2) % groups, turned, ninth),
            )

    on_each_core(run, SECOND)


def cross_best(best, labels, other_labels, arrived, others):
    slots = arrived.shape[0]
    half = slots // 2
    best, gained = pl.pallas_call(
        first_kernel,
        out_shape=(
            jax.ShapeDtypeStruct(best.shape, jnp.float32),
            jax.ShapeDtypeStruct((1, half), jnp.float32),
        ),
        compiler_params=params(),
    )(best, labels, other_labels, arrived, others[0])
    return pl.pallas_call(
        second_kernel,
        out_shape=jax.ShapeDtypeStruct((slots // CAP, LANES), jnp.float32),
        compiler_params=params(),
    )(best, gained, labels, other_labels, arrived, others[1])


def lookup_kernel(members, table_ref, dest_ref, out_ref):
    devices = table_ref.shape[0]
    rows = dest_ref.shape[1]
    mine = lax.axis_index("grp")
    groups = devices // members
    table = table_ref[...]
    turned = pltpu.roll(table, LANES // 2, 1)
    core = iota((devices, LANES), 0) // groups % 2
    other = jnp.where(
        core == 0, pltpu.roll(turned, devices - groups, 0), pltpu.roll(turned, groups, 0)
    )
    window = iota((devices, LANES), 1) // CAP
    table = jnp.where(window == mine, jnp.maximum(table, other), table)
    group, member, row = place(dest_ref[...], members)
    pick = ones_where(iota((devices, rows), 0) == member * groups + group)
    parts = []
    left = table.T
    for _ in range(3):
        parts.append(left.astype(jnp.bfloat16))
        left = left - parts[-1].astype(jnp.float32)
    found = dot(jnp.concatenate(parts, axis=1), jnp.concatenate([pick] * 3, axis=0))
    lane = jnp.where(row < CAP, CAP * mine + row, ninth_lane(mine, lax.axis_index("mem")))
    out_ref[...] = jnp.max(
        jnp.where(iota((LANES, rows), 0) == lane, found, -1.0), axis=0, keepdims=True
    )


def lookup(table, dest, members):
    rows = dest.shape[0]
    return pl.pallas_call(
        functools.partial(lookup_kernel, members),
        out_shape=jax.ShapeDtypeStruct((1, rows), jnp.float32),
        compiler_params=params(),
    )(table, dest.reshape(1, rows)).reshape(rows)


def shards(embeds, cluster, dest):
    members = lax.axis_size("mem")
    devices = lax.axis_size("grp") * members
    width = embeds.shape[1]
    slots = devices * CAP
    outgoing = pack(embeds, cluster, dest, slots, members)
    arrived = lax.all_to_all(
        outgoing.reshape(devices, CAP, width + LANES),
        ("mem", "grp"),
        split_axis=0,
        concat_axis=0,
        tiled=True,
    ).reshape(slots, width + LANES)
    half = slots // 2
    others = [
        lax.ppermute(arrived[first : first + half, :width], "mem", swap_cores(members))
        for first in (0, half)
    ]
    best, labels, other_labels = own_best(arrived)
    table = cross_best(best, labels, other_labels, arrived, others)
    returned = lax.all_to_all(
        table.reshape(devices, 1, LANES),
        ("mem", "grp"),
        split_axis=0,
        concat_axis=0,
        tiled=True,
    ).reshape(devices, LANES)
    return lookup(returned, dest, members)


def solution(mesh):
    placed = (P(("grp", "mem"), None), P(("grp", "mem")), P(("grp", "mem")))
    return jax.shard_map(
        shards, mesh=mesh, in_specs=placed, out_specs=P(("grp", "mem")), check_vma=False
    )
```

```python
import functools

import jax
import jax.numpy as jnp
from jax import lax
from jax.experimental import pallas as pl
from jax.experimental.pallas import tpu as pltpu
from jax.sharding import PartitionSpec as P

CAP = 8
SHARED = 2
KEPT = CAP - SHARED
SPLIT = KEPT // 2
LANES = 128
OTHERS = 2 * CAP
VMEM_LIMIT = 48 * 1024 * 1024


def place(dest, members):
    owner = dest // CAP
    group = owner // members
    member = owner % members
    column = dest % CAP
    shared = member * SHARED + column
    index = column - SHARED
    third = member % 3
    halved = third == 2
    spread = column < SHARED
    core = jnp.where(
        spread, shared // CAP, jnp.where(halved, index // SPLIT, third)
    )
    chip = jnp.where(spread, 0, 1 + member // 3)
    row = jnp.where(
        spread, shared % CAP, jnp.where(halved, index % SPLIT, index + SPLIT)
    )
    return group, 2 * chip + core, row


def swap_cores(members):
    return [(member, member ^ 1) for member in range(members)]


def params():
    return pltpu.CompilerParams(vmem_limit_bytes=VMEM_LIMIT)


def iota(shape, axis):
    return lax.broadcasted_iota(jnp.int32, shape, axis)


def dot(a, b):
    return jnp.dot(a, b, preferred_element_type=jnp.float32)


def dot_t(a, b):
    return lax.dot_general(a, b, (((1,), (1,)), ((), ())), preferred_element_type=jnp.float32)


def ones_where(mask):
    return jnp.where(mask, 1.0, 0.0).astype(jnp.bfloat16)


def label_lines(lane, label):
    return jnp.where(iota((LANES, lane.shape[1]), 0) == lane, label, 0.0).astype(jnp.bfloat16)


def pack_kernel(
    members, embeds_hbm, cluster_hbm, dest_hbm, out_ref,
    embeds_ref, cluster_ref, dest_ref, unit_ref, last_ref, sems,
):
    rows, width = embeds_ref.shape
    slots = out_ref.shape[0]
    devices = slots // CAP
    block = 256
    copies = [
        pltpu.make_async_copy(source, target, sems.at[index])
        for index, (source, target) in enumerate(
            ((dest_hbm, dest_ref), (cluster_hbm, cluster_ref), (embeds_hbm, embeds_ref))
        )
    ]
    for copy in copies:
        copy.start()
    copies[0].wait()
    copies[1].wait()
    group, member, row = place(dest_ref[...], members)
    device = member * (devices // members) + group
    slot = jnp.where(row < CAP, device * CAP + row, -1)
    picks = [ones_where(b + iota((block, rows), 0) == slot) for b in range(0, slots, block)]
    here = iota((devices, rows), 0) == device
    pick_ninth = ones_where(here & (row == CAP))
    label = (cluster_ref[...] + 1).astype(jnp.float32)
    labels = dot_t(ones_where(here), label_lines(row, label))
    other = (member ^ 1) * (devices // members) + group
    here_other = ones_where(iota((devices, rows), 0) == other)
    labels += dot_t(here_other, label_lines(row + OTHERS, label))
    for piece in range(width // LANES, CAP):
        last_ref[pl.ds(piece, devices, stride=CAP), :] = labels

    copies[2].wait()
    values = embeds_ref[...].astype(jnp.float32)
    total = jnp.sum(values * values, axis=1, keepdims=True)
    unit_ref[...] = (values * lax.rsqrt(total + 1e-06)).astype(jnp.bfloat16)
    for b, pick in enumerate(picks):
        out_ref[b * block : (b + 1) * block, :width] = dot(pick, unit_ref[...]).astype(
            jnp.bfloat16
        )
    ninth = dot(pick_ninth, unit_ref[...])
    for piece in range(width // LANES):
        last_ref[pl.ds(piece, devices, stride=CAP), :] = ninth[
            :, piece * LANES : (piece + 1) * LANES
        ]
    out_ref[:, width:] = last_ref[...].astype(jnp.bfloat16)


def pack(embeds, cluster, dest, slots, members):
    rows, width = embeds.shape
    operands = [
        pltpu.with_memory_space_constraint(operand, pltpu.HBM)
        for operand in (embeds, cluster.reshape(1, rows), dest.reshape(1, rows))
    ]
    return pl.pallas_call(
        functools.partial(pack_kernel, members),
        out_shape=jax.ShapeDtypeStruct((slots, width + LANES), jnp.bfloat16),
        in_specs=[pl.BlockSpec(memory_space=pltpu.HBM)] * 3,
        scratch_shapes=[
            pltpu.VMEM((rows, width), jnp.bfloat16),
            pltpu.VMEM((1, rows), jnp.int32),
            pltpu.VMEM((1, rows), jnp.int32),
            pltpu.VMEM((rows, width), jnp.bfloat16),
            pltpu.VMEM((slots, LANES), jnp.float32),
            pltpu.SemaphoreType.DMA((3,)),
        ],
        compiler_params=params(),
    )(*operands)


def ninth_lane(group, member):
    return CAP * ((group + 1) % (LANES // CAP)) + member


def repeat_lines(labels, slots):
    shape = (slots, labels.shape[0])
    return dot(ones_where(iota(shape, 0) // CAP == iota(shape, 1)), labels)


def only_own(lines, first):
    own = iota(lines.shape, 1) == first + iota(lines.shape, 0) % CAP
    return jnp.where(own, lines, 0.0)


def in_every_lane(spots):
    return jnp.broadcast_to(jnp.sum(spots, axis=1, keepdims=True), spots.shape)


def masked(scores, key_labels, query_labels, skip=False):
    count, size = scores.shape
    tiles = []
    for lane in range(0, size, LANES):
        same = key_labels == query_labels[:, lane : lane + LANES]
        if skip:
            same = same & (iota((count, LANES), 0) != iota((count, LANES), 1) + lane)
        tiles.append(jnp.where(same, scores[:, lane : lane + LANES], -1.0))
    return jnp.concatenate(tiles, axis=1)


def widen(widest, scores):
    for lane in range(0, scores.shape[1], LANES):
        widest = jnp.maximum(widest, scores[:, lane : lane + LANES])
    return widest


def across(widest):
    return jnp.concatenate(
        [
            jnp.max(widest[j : j + LANES].T, axis=0, keepdims=True)
            for j in range(0, widest.shape[0], LANES)
        ],
        axis=1,
    )


def own_kernel(
    rows_ref, best_ref, labels_ref, others_ref, last_ref, ninth_ref, column_ref
):
    slots, wide = rows_ref.shape
    width = wide - LANES
    sources = slots // CAP
    def run(with_ninth):
        last_ref[...] = rows_ref[:, width:].astype(jnp.float32)
        if with_ninth:
            for piece in range(width // LANES):
                ninth_ref[:, piece * LANES : (piece + 1) * LANES] = last_ref[
                    pl.ds(piece, sources, stride=CAP), :
                ].astype(jnp.bfloat16)
        labels = last_ref[pl.ds(width // LANES, sources, stride=CAP), :].astype(jnp.bfloat16)
        lines = repeat_lines(labels, slots)
        spots = only_own(lines, 0)
        others_ref[...] = in_every_lane(only_own(lines, OTHERS))
        if with_ninth:
            groups = LANES // CAP
            source = iota((sources, LANES), 1)
            order = ones_where(
                iota((sources, LANES), 0) == ninth_lane(source % groups, source // groups)
            )
            ninth_ref[...] = dot(order, ninth_ref[...]).astype(jnp.bfloat16)
            labels = dot(order, labels).astype(jnp.bfloat16)
        ones = jnp.ones((LANES, LANES), jnp.bfloat16)
        column_ref[:slots, :] = in_every_lane(spots)
        at_ninth = ones_where(iota((LANES, LANES), 0) == CAP)
        column_ref[slots:, :] = dot(labels, at_ninth)
        at_ninth = ones_where(iota((CAP, LANES), 1) == CAP)
        row_labels = jnp.concatenate(
            [dot_t(ones[:CAP], spots.astype(jnp.bfloat16)), dot_t(at_ninth, labels)], axis=1
        )
        labels_ref[...] = row_labels

        block = 256
        starts = list(range(0, slots, block))
        sizes = [block] * len(starts)
        if with_ninth:
            starts.append(slots)
            sizes.append(sources)
        else:
            best_ref[:, slots:] = jnp.full((1, sources), -1.0, jnp.float32)

        def read(i):
            if starts[i] == slots:
                return ninth_ref[...]
            return rows_ref[starts[i] : starts[i] + block, :width]

        best = [jnp.full((1, size), -1.0, jnp.float32) for size in sizes]
        for k, (key, count) in enumerate(zip(starts, sizes)):
            widest = jnp.full((count, LANES), -1.0, jnp.float32)
            keys = read(k)
            for q in range(k, len(starts)):
                query, size = starts[q], sizes[q]
                scores = masked(
                    dot_t(keys, read(q)),
                    column_ref[key : key + count, :],
                    row_labels[:1, query : query + size],
                    q == k,
                )
                best[q] = jnp.maximum(best[q], jnp.max(scores, axis=0, keepdims=True))
                if q > k:
                    widest = widen(widest, scores)
            if k + 1 < len(starts):
                best[k] = jnp.maximum(best[k], across(widest))
            best_ref[:, key : key + count] = best[k]

    spread = lax.axis_index("mem") < 2
    pl.when(spread)(lambda: run(False))
    pl.when(jnp.logical_not(spread))(lambda: run(True))


def own_best(arrived):
    slots, wide = arrived.shape
    count = slots + slots // CAP
    return pl.pallas_call(
        own_kernel,
        out_shape=(
            jax.ShapeDtypeStruct((1, count), jnp.float32),
            jax.ShapeDtypeStruct((CAP, count), jnp.float32),
            jax.ShapeDtypeStruct((slots, LANES), jnp.float32),
        ),
        scratch_shapes=[
            pltpu.VMEM((slots, LANES), jnp.float32),
            pltpu.VMEM((slots // CAP, wide - LANES), jnp.bfloat16),
            pltpu.VMEM((count, LANES), jnp.float32),
        ],
        compiler_params=params(),
    )(arrived)


FIRST = ({0: (0, 2, 3), 1: (0, 2, 3)}, {0: (2, 3), 1: (0, 1, 2, 3)})
SECOND = ({2: (2,), 3: (2,)}, {3: (2, 3)})
BLOCKS = 4


def on_each_core(run, plans):
    member = lax.axis_index("mem")
    core = member % 2
    alone = member // 2 == lax.axis_size("mem") // 2 - 1
    pl.when(alone)(lambda: run({}))
    for index, plan in enumerate(plans):
        pl.when(jnp.logical_not(alone) & (core == index))(functools.partial(run, plan))


def meet(plan, best_ref, labels_ref, others_ref, rows_ref, other_ref):
    slots = rows_ref.shape[0]
    half, width = other_ref.shape
    block = slots // BLOCKS
    own = [best_ref[:, q * block : (q + 1) * block] for q in range(BLOCKS)]
    gained = [jnp.full((1, block), -1.0, jnp.float32)] * (BLOCKS // 2)
    for k, queries in plan.items():
        first = k * block % half
        keys = other_ref[first : first + block, :]
        key_labels = others_ref[k * block : (k + 1) * block, :]
        widest = jnp.full((block, LANES), -1.0, jnp.float32)
        for q in queries:
            scores = masked(
                dot_t(keys, rows_ref[q * block : (q + 1) * block, :width]),
                key_labels,
                labels_ref[:1, q * block : (q + 1) * block],
            )
            own[q] = jnp.maximum(own[q], jnp.max(scores, axis=0, keepdims=True))
            widest = widen(widest, scores)
        gained[k % (BLOCKS // 2)] = across(widest)
    return jnp.concatenate(own, axis=1), jnp.concatenate(gained, axis=1)


def first_kernel(
    best_ref, labels_ref, others_ref, rows_ref, other_ref, out_ref, gained_ref
):
    slots = rows_ref.shape[0]

    def run(plan):
        own, gained = meet(plan, best_ref, labels_ref, others_ref, rows_ref, other_ref)
        out_ref[:, :slots] = own
        out_ref[:, slots:] = best_ref[:, slots:]
        gained_ref[...] = gained

    on_each_core(run, FIRST)


def second_kernel(
    best_ref, gained_ref, labels_ref, others_ref, rows_ref, other_ref, out_ref
):
    slots = rows_ref.shape[0]
    groups = LANES // CAP
    shape = (groups, LANES)

    def run(plan):
        own, gained = meet(plan, best_ref, labels_ref, others_ref, rows_ref, other_ref)
        gained = jnp.concatenate([gained_ref[...], gained], axis=1)
        window = iota(shape, 1) // CAP
        mine = iota(shape, 0)
        ninth = jnp.broadcast_to(best_ref[:, slots:], shape)
        for first in range(0, slots, LANES):
            tile = slice(first, first + LANES)
            turned = pltpu.roll(jnp.broadcast_to(gained[:, tile], shape), LANES // 2, 1)
            out_ref[first // CAP : first // CAP + groups, :] = jnp.where(
                window == mine,
                jnp.broadcast_to(own[:, tile], shape),
                jnp.where(window == (mine + groups // 2) % groups, turned, ninth),
            )

    on_each_core(run, SECOND)


def cross_best(best, labels, other_labels, arrived, others):
    slots = arrived.shape[0]
    half = slots // 2
    best, gained = pl.pallas_call(
        first_kernel,
        out_shape=(
            jax.ShapeDtypeStruct(best.shape, jnp.float32),
            jax.ShapeDtypeStruct((1, half), jnp.float32),
        ),
        compiler_params=params(),
    )(best, labels, other_labels, arrived, others[0])
    return pl.pallas_call(
        second_kernel,
        out_shape=jax.ShapeDtypeStruct((slots // CAP, LANES), jnp.float32),
        compiler_params=params(),
    )(best, gained, labels, other_labels, arrived, others[1])


def lookup_kernel(members, table_ref, dest_ref, out_ref):
    devices = table_ref.shape[0]
    rows = dest_ref.shape[1]
    mine = lax.axis_index("grp")
    groups = devices // members
    table = table_ref[...]
    turned = pltpu.roll(table, LANES // 2, 1)
    core = iota((devices, LANES), 0) // groups % 2
    other = jnp.where(
        core == 0, pltpu.roll(turned, devices - groups, 0), pltpu.roll(turned, groups, 0)
    )
    window = iota((devices, LANES), 1) // CAP
    table = jnp.where(window == mine, jnp.maximum(table, other), table)
    group, member, row = place(dest_ref[...], members)
    pick = ones_where(iota((devices, rows), 0) == member * groups + group)
    parts = []
    left = table.T
    for _ in range(3):
        parts.append(left.astype(jnp.bfloat16))
        left = left - parts[-1].astype(jnp.float32)
    found = dot(jnp.concatenate(parts, axis=1), jnp.concatenate([pick] * 3, axis=0))
    lane = jnp.where(row < CAP, CAP * mine + row, ninth_lane(mine, lax.axis_index("mem")))
    out_ref[...] = jnp.max(
        jnp.where(iota((LANES, rows), 0) == lane, found, -1.0), axis=0, keepdims=True
    )


def lookup(table, dest, members):
    rows = dest.shape[0]
    return pl.pallas_call(
        functools.partial(lookup_kernel, members),
        out_shape=jax.ShapeDtypeStruct((1, rows), jnp.float32),
        compiler_params=params(),
    )(table, dest.reshape(1, rows)).reshape(rows)


def shards(embeds, cluster, dest):
    members = lax.axis_size("mem")
    devices = lax.axis_size("grp") * members
    width = embeds.shape[1]
    slots = devices * CAP
    outgoing = pack(embeds, cluster, dest, slots, members)
    arrived = lax.all_to_all(
        outgoing.reshape(devices, CAP, width + LANES),
        ("mem", "grp"),
        split_axis=0,
        concat_axis=0,
        tiled=True,
    ).reshape(slots, width + LANES)
    half = slots // 2
    others = [
        lax.ppermute(arrived[first : first + half, :width], "mem", swap_cores(members))
        for first in (0, half)
    ]
    best, labels, other_labels = own_best(arrived)
    table = cross_best(best, labels, other_labels, arrived, others)
    returned = lax.all_to_all(
        table.reshape(devices, 1, LANES),
        ("mem", "grp"),
        split_axis=0,
        concat_axis=0,
        tiled=True,
    ).reshape(devices, LANES)
    return lookup(returned, dest, members)


def solution(mesh):
    placed = (P(("grp", "mem"), None), P(("grp", "mem")), P(("grp", "mem")))
    return jax.shard_map(
        shards, mesh=mesh, in_specs=placed, out_specs=P(("grp", "mem")), check_vma=False
    )
```

```python
import functools

import jax
import jax.numpy as jnp
from jax import lax
from jax.experimental import pallas as pl
from jax.experimental.pallas import tpu as pltpu
from jax.sharding import PartitionSpec as P

CAP = 8
SHARED = 2
KEPT = CAP - SHARED
SPLIT = KEPT // 2
LANES = 128
OTHERS = 2 * CAP
VMEM_LIMIT = 48 * 1024 * 1024


def place(dest, members):
    owner = dest // CAP
    group = owner // members
    member = owner % members
    column = dest % CAP
    shared = member * SHARED + column
    index = column - SHARED
    third = member % 3
    halved = third == 2
    spread = column < SHARED
    core = jnp.where(
        spread, shared // CAP, jnp.where(halved, index // SPLIT, third)
    )
    chip = jnp.where(spread, 0, 1 + member // 3)
    row = jnp.where(
        spread, shared % CAP, jnp.where(halved, index % SPLIT, index + SPLIT)
    )
    return group, 2 * chip + core, row


def swap_cores(members):
    return [(member, member ^ 1) for member in range(members)]


def params():
    return pltpu.CompilerParams(vmem_limit_bytes=VMEM_LIMIT)


def iota(shape, axis):
    return lax.broadcasted_iota(jnp.int32, shape, axis)


def dot(a, b):
    return jnp.dot(a, b, preferred_element_type=jnp.float32)


def dot_t(a, b):
    return lax.dot_general(a, b, (((1,), (1,)), ((), ())), preferred_element_type=jnp.float32)


def ones_where(mask):
    return jnp.where(mask, 1.0, 0.0).astype(jnp.bfloat16)


def label_lines(lane, label):
    return jnp.where(iota((LANES, lane.shape[1]), 0) == lane, label, 0.0).astype(jnp.bfloat16)


def pack_kernel(
    members, embeds_hbm, cluster_hbm, dest_hbm, out_ref, device_ref, lane_ref,
    embeds_ref, cluster_ref, dest_ref, unit_ref, last_ref, sems,
):
    rows, width = embeds_ref.shape
    slots = out_ref.shape[0]
    devices = slots // CAP
    block = 256
    copies = [
        pltpu.make_async_copy(source, target, sems.at[index])
        for index, (source, target) in enumerate(
            ((dest_hbm, dest_ref), (cluster_hbm, cluster_ref), (embeds_hbm, embeds_ref))
        )
    ]
    for copy in copies:
        copy.start()
    copies[0].wait()
    copies[1].wait()
    group, member, row = place(dest_ref[...], members)
    device = member * (devices // members) + group
    slot = jnp.where(row < CAP, device * CAP + row, -1)
    picks = [ones_where(b + iota((block, rows), 0) == slot) for b in range(0, slots, block)]
    here = iota((devices, rows), 0) == device
    pick_ninth = ones_where(here & (row == CAP))
    device_ref[...] = ones_where(here)
    mine, seat = lax.axis_index("grp"), lax.axis_index("mem")
    lane_ref[...] = jnp.where(row < CAP, CAP * mine + row, ninth_lane(mine, seat))
    label = (cluster_ref[...] + 1).astype(jnp.float32)
    labels = dot_t(device_ref[...], label_lines(row, label))
    other = (member ^ 1) * (devices // members) + group
    here_other = ones_where(iota((devices, rows), 0) == other)
    labels += dot_t(here_other, label_lines(row + OTHERS, label))
    for piece in range(width // LANES, CAP):
        last_ref[pl.ds(piece, devices, stride=CAP), :] = labels

    copies[2].wait()
    values = embeds_ref[...].astype(jnp.float32)
    total = jnp.sum(values * values, axis=1, keepdims=True)
    unit_ref[...] = (values * lax.rsqrt(total + 1e-06)).astype(jnp.bfloat16)
    for b, pick in enumerate(picks):
        out_ref[b * block : (b + 1) * block, :width] = dot(pick, unit_ref[...]).astype(
            jnp.bfloat16
        )
    ninth = dot(pick_ninth, unit_ref[...])
    for piece in range(width // LANES):
        last_ref[pl.ds(piece, devices, stride=CAP), :] = ninth[
            :, piece * LANES : (piece + 1) * LANES
        ]
    out_ref[:, width:] = last_ref[...].astype(jnp.bfloat16)


def pack(embeds, cluster, dest, slots, members):
    rows, width = embeds.shape
    operands = [
        pltpu.with_memory_space_constraint(operand, pltpu.HBM)
        for operand in (embeds, cluster.reshape(1, rows), dest.reshape(1, rows))
    ]
    return pl.pallas_call(
        functools.partial(pack_kernel, members),
        out_shape=(
            jax.ShapeDtypeStruct((slots, width + LANES), jnp.bfloat16),
            jax.ShapeDtypeStruct((slots // CAP, rows), jnp.bfloat16),
            jax.ShapeDtypeStruct((1, rows), jnp.int32),
        ),
        in_specs=[pl.BlockSpec(memory_space=pltpu.HBM)] * 3,
        scratch_shapes=[
            pltpu.VMEM((rows, width), jnp.bfloat16),
            pltpu.VMEM((1, rows), jnp.int32),
            pltpu.VMEM((1, rows), jnp.int32),
            pltpu.VMEM((rows, width), jnp.bfloat16),
            pltpu.VMEM((slots, LANES), jnp.float32),
            pltpu.SemaphoreType.DMA((3,)),
        ],
        compiler_params=params(),
    )(*operands)


def ninth_lane(group, member):
    return CAP * ((group + 1) % (LANES // CAP)) + member


def repeat_lines(labels, slots):
    shape = (slots, labels.shape[0])
    return dot(ones_where(iota(shape, 0) // CAP == iota(shape, 1)), labels)


def only_own(lines, first):
    own = iota(lines.shape, 1) == first + iota(lines.shape, 0) % CAP
    return jnp.where(own, lines, 0.0)


def in_every_lane(spots):
    return jnp.broadcast_to(jnp.sum(spots, axis=1, keepdims=True), spots.shape)


def masked(scores, key_labels, query_labels, skip=False):
    count, size = scores.shape
    tiles = []
    for lane in range(0, size, LANES):
        same = key_labels == query_labels[:, lane : lane + LANES]
        if skip:
            same = same & (iota((count, LANES), 0) != iota((count, LANES), 1) + lane)
        tiles.append(jnp.where(same, scores[:, lane : lane + LANES], -1.0))
    return jnp.concatenate(tiles, axis=1)


def widen(widest, scores):
    for lane in range(0, scores.shape[1], LANES):
        widest = jnp.maximum(widest, scores[:, lane : lane + LANES])
    return widest


def across(widest):
    return jnp.concatenate(
        [
            jnp.max(widest[j : j + LANES].T, axis=0, keepdims=True)
            for j in range(0, widest.shape[0], LANES)
        ],
        axis=1,
    )


def own_kernel(
    rows_ref, best_ref, labels_ref, others_ref, last_ref, ninth_ref, column_ref
):
    slots, wide = rows_ref.shape
    width = wide - LANES
    sources = slots // CAP
    last_ref[...] = rows_ref[:, width:].astype(jnp.float32)
    for piece in range(width // LANES):
        ninth_ref[:, piece * LANES : (piece + 1) * LANES] = last_ref[
            pl.ds(piece, sources, stride=CAP), :
        ].astype(jnp.bfloat16)
    labels = last_ref[pl.ds(width // LANES, sources, stride=CAP), :].astype(jnp.bfloat16)
    lines = repeat_lines(labels, slots)
    spots = only_own(lines, 0)
    others_ref[...] = in_every_lane(only_own(lines, OTHERS))
    groups = LANES // CAP
    source = iota((sources, LANES), 1)
    order = ones_where(
        iota((sources, LANES), 0) == ninth_lane(source % groups, source // groups)
    )
    ninth_ref[...] = dot(order, ninth_ref[...]).astype(jnp.bfloat16)
    labels = dot(order, labels).astype(jnp.bfloat16)
    ones = jnp.ones((LANES, LANES), jnp.bfloat16)
    column_ref[:slots, :] = in_every_lane(spots)
    at_ninth = ones_where(iota((LANES, LANES), 0) == CAP)
    column_ref[slots:, :] = dot(labels, at_ninth)
    at_ninth = ones_where(iota((CAP, LANES), 1) == CAP)
    row_labels = jnp.concatenate(
        [dot_t(ones[:CAP], spots.astype(jnp.bfloat16)), dot_t(at_ninth, labels)], axis=1
    )
    labels_ref[...] = row_labels

    block = 256
    starts = list(range(0, slots, block)) + [slots]
    sizes = [block] * (slots // block) + [sources]

    def read(i):
        if starts[i] == slots:
            return ninth_ref[...]
        return rows_ref[starts[i] : starts[i] + block, :width]

    best = [jnp.full((1, size), -1.0, jnp.float32) for size in sizes]
    for k, (key, count) in enumerate(zip(starts, sizes)):
        widest = jnp.full((count, LANES), -1.0, jnp.float32)
        keys = read(k)
        for q in range(k, len(starts)):
            query, size = starts[q], sizes[q]
            scores = masked(
                dot_t(keys, read(q)),
                column_ref[key : key + count, :],
                row_labels[:1, query : query + size],
                q == k,
            )
            best[q] = jnp.maximum(best[q], jnp.max(scores, axis=0, keepdims=True))
            if q > k:
                widest = widen(widest, scores)
        if k + 1 < len(starts):
            best[k] = jnp.maximum(best[k], across(widest))
        best_ref[:, key : key + count] = best[k]


def own_best(arrived):
    slots, wide = arrived.shape
    count = slots + slots // CAP
    return pl.pallas_call(
        own_kernel,
        out_shape=(
            jax.ShapeDtypeStruct((1, count), jnp.float32),
            jax.ShapeDtypeStruct((CAP, count), jnp.float32),
            jax.ShapeDtypeStruct((slots, LANES), jnp.float32),
        ),
        scratch_shapes=[
            pltpu.VMEM((slots, LANES), jnp.float32),
            pltpu.VMEM((slots // CAP, wide - LANES), jnp.bfloat16),
            pltpu.VMEM((count, LANES), jnp.float32),
        ],
        compiler_params=params(),
    )(arrived)


FIRST = ({0: (0, 2, 3), 1: (0, 2, 3)}, {0: (2, 3), 1: (0, 1, 2, 3)})
SECOND = ({2: (2,), 3: (2,)}, {3: (2, 3)})
BLOCKS = 4


def on_each_core(run, plans):
    member = lax.axis_index("mem")
    core = member % 2
    alone = member // 2 == lax.axis_size("mem") // 2 - 1
    pl.when(alone)(lambda: run({}))
    for index, plan in enumerate(plans):
        pl.when(jnp.logical_not(alone) & (core == index))(functools.partial(run, plan))


def meet(plan, best_ref, labels_ref, others_ref, rows_ref, other_ref):
    slots = rows_ref.shape[0]
    half, width = other_ref.shape
    block = slots // BLOCKS
    own = [best_ref[:, q * block : (q + 1) * block] for q in range(BLOCKS)]
    gained = [jnp.full((1, block), -1.0, jnp.float32)] * (BLOCKS // 2)
    for k, queries in plan.items():
        first = k * block % half
        keys = other_ref[first : first + block, :]
        key_labels = others_ref[k * block : (k + 1) * block, :]
        widest = jnp.full((block, LANES), -1.0, jnp.float32)
        for q in queries:
            scores = masked(
                dot_t(keys, rows_ref[q * block : (q + 1) * block, :width]),
                key_labels,
                labels_ref[:1, q * block : (q + 1) * block],
            )
            own[q] = jnp.maximum(own[q], jnp.max(scores, axis=0, keepdims=True))
            widest = widen(widest, scores)
        gained[k % (BLOCKS // 2)] = across(widest)
    return jnp.concatenate(own, axis=1), jnp.concatenate(gained, axis=1)


def first_kernel(
    best_ref, labels_ref, others_ref, rows_ref, other_ref, out_ref, gained_ref
):
    slots = rows_ref.shape[0]

    def run(plan):
        own, gained = meet(plan, best_ref, labels_ref, others_ref, rows_ref, other_ref)
        out_ref[:, :slots] = own
        out_ref[:, slots:] = best_ref[:, slots:]
        gained_ref[...] = gained

    on_each_core(run, FIRST)


def second_kernel(
    best_ref, gained_ref, labels_ref, others_ref, rows_ref, other_ref, out_ref
):
    slots = rows_ref.shape[0]
    groups = LANES // CAP
    shape = (groups, LANES)

    def run(plan):
        own, gained = meet(plan, best_ref, labels_ref, others_ref, rows_ref, other_ref)
        gained = jnp.concatenate([gained_ref[...], gained], axis=1)
        window = iota(shape, 1) // CAP
        mine = iota(shape, 0)
        ninth = jnp.broadcast_to(best_ref[:, slots:], shape)
        for first in range(0, slots, LANES):
            tile = slice(first, first + LANES)
            turned = pltpu.roll(jnp.broadcast_to(gained[:, tile], shape), LANES // 2, 1)
            out_ref[first // CAP : first // CAP + groups, :] = jnp.where(
                window == mine,
                jnp.broadcast_to(own[:, tile], shape),
                jnp.where(window == (mine + groups // 2) % groups, turned, ninth),
            )

    on_each_core(run, SECOND)


def cross_best(best, labels, other_labels, arrived, others):
    slots = arrived.shape[0]
    half = slots // 2
    best, gained = pl.pallas_call(
        first_kernel,
        out_shape=(
            jax.ShapeDtypeStruct(best.shape, jnp.float32),
            jax.ShapeDtypeStruct((1, half), jnp.float32),
        ),
        compiler_params=params(),
    )(best, labels, other_labels, arrived, others[0])
    return pl.pallas_call(
        second_kernel,
        out_shape=jax.ShapeDtypeStruct((slots // CAP, LANES), jnp.float32),
        compiler_params=params(),
    )(best, gained, labels, other_labels, arrived, others[1])


def lookup_kernel(members, table_ref, device_ref, lane_ref, out_ref):
    devices = table_ref.shape[0]
    rows = lane_ref.shape[1]
    mine = lax.axis_index("grp")
    groups = devices // members
    table = table_ref[...]
    turned = pltpu.roll(table, LANES // 2, 1)
    core = iota((devices, LANES), 0) // groups % 2
    other = jnp.where(
        core == 0, pltpu.roll(turned, devices - groups, 0), pltpu.roll(turned, groups, 0)
    )
    window = iota((devices, LANES), 1) // CAP
    table = jnp.where(window == mine, jnp.maximum(table, other), table)
    pick = device_ref[...]
    parts = []
    left = table.T
    for _ in range(3):
        parts.append(left.astype(jnp.bfloat16))
        left = left - parts[-1].astype(jnp.float32)
    found = dot(jnp.concatenate(parts, axis=1), jnp.concatenate([pick] * 3, axis=0))
    out_ref[...] = jnp.max(
        jnp.where(iota((LANES, rows), 0) == lane_ref[...], found, -1.0), axis=0, keepdims=True
    )


def lookup(table, device, lane, members):
    rows = lane.shape[1]
    return pl.pallas_call(
        functools.partial(lookup_kernel, members),
        out_shape=jax.ShapeDtypeStruct((1, rows), jnp.float32),
        compiler_params=params(),
    )(table, device, lane).reshape(rows)


def shards(embeds, cluster, dest):
    members = lax.axis_size("mem")
    devices = lax.axis_size("grp") * members
    width = embeds.shape[1]
    slots = devices * CAP
    outgoing, device, lane = pack(embeds, cluster, dest, slots, members)
    arrived = lax.all_to_all(
        outgoing.reshape(devices, CAP, width + LANES),
        ("mem", "grp"),
        split_axis=0,
        concat_axis=0,
        tiled=True,
    ).reshape(slots, width + LANES)
    half = slots // 2
    others = [
        lax.ppermute(arrived[first : first + half, :width], "mem", swap_cores(members))
        for first in (0, half)
    ]
    best, labels, other_labels = own_best(arrived)
    table = cross_best(best, labels, other_labels, arrived, others)
    returned = lax.all_to_all(
        table.reshape(devices, 1, LANES),
        ("mem", "grp"),
        split_axis=0,
        concat_axis=0,
        tiled=True,
    ).reshape(devices, LANES)
    return lookup(returned, device, lane, members)


def solution(mesh):
    placed = (P(("grp", "mem"), None), P(("grp", "mem")), P(("grp", "mem")))
    return jax.shard_map(
        shards, mesh=mesh, in_specs=placed, out_specs=P(("grp", "mem")), check_vma=False
    )
```
